256 devices in a mesh: gx: 32 (over x, z), gy: 8 (over y, core).
Axes of the slice: x: 4, y: 4, z: 8, core: 2. Of those that a mesh axis runs over, the one named last changes fastest.
Arguments:
- vorticity: float32 [8, 512, 1024], P(None, 'gx', 'gy'), may hold values from -6 to 6
- metric: float32 [3, 8, 512, 1024], P(None, None, 'gx', 'gy'), may hold values from 0.25 to 4
Outputs:
- stream: float32 [8, 512, 1024], P(None, 'gx', 'gy')
- residual: float32 [8, 512, 1024], P(None, 'gx', 'gy')
The draws below stay inside these ranges and needn't reach their ends.
All inputs are finite; a program needn't handle non-finite values.
Results may differ from the reference program's by a relative error of at most 0.0003.
Values sent between devices are 32-bit elements; how exact they have to be, the bound alone decides.
A program may use at most 64 MiB of HBM per device.

```python
import math
import jax
import jax.numpy as jnp

Z = 8
LEVELS = 5
CSWEEPS = 8
NX = 512
NY = 1024


def block_scale(own_key, dims, cuts, smallest, high):
    factor_of, own = 1.0, jax.random.fold_in(own_key, 6)
    for position, blocks in cuts:
        draws = jnp.exp(jax.random.uniform(jax.random.fold_in(own, position), (blocks,), jnp.float32, smallest / len(cuts), high / len(cuts)))
        factor_of = factor_of * jnp.repeat(draws, dims[position] // blocks).reshape([-1 if axis == position else 1 for axis in range(len(dims))])
    return factor_of


def bell_draw(key, extent, deviation, bound, shards=(), kind=jnp.bfloat16):
    drawn = jax.random.normal(key, extent, jnp.float32) * deviation
    if len(shards) > 0:
        drawn = block_scale(key, extent, shards, -0.22, 0.18) * drawn
    return jnp.clip(drawn, min=-bound, max=bound).astype(kind)


def setup_inputs(seed: int = 0) -> dict:
    seeds = jax.random.split(jax.random.key(seed), 3)
    return {
        "vorticity": bell_draw(seeds[0], (Z, NX, NY), 1.0, 6.0, ((1, 32), (2, 8)), jnp.float32),
        "metric": jnp.clip(jnp.exp(math.log(4.0) - 2.7725887 * jax.random.uniform(seeds[1], (3, Z, NX, NY), jnp.float32) ** block_scale(seeds[1], (3, Z, NX, NY), ((2, 32), (3, 8)), -0.2, 0.2)), 0.25, 4.0),
    }


omega_relax = 0.8


def coarsen(values):
    shape = values.shape
    grouped = values.reshape(shape[:-2] + (shape[-2] // 2, 2, shape[-1] // 2, 2))
    return grouped.mean(axis=(-3, -1))


def refine(values):
    return jnp.repeat(jnp.repeat(values, 2, axis=1), 2, axis=2)


def face_coeffs(metric, padded, level_no):
    scale = 0.25 ** level_no
    span_scale = 0.25 ** (LEVELS - 1)
    m_x = metric[0]
    m_y = metric[1]
    m_z = metric[2]
    c_east = 0.5 * (m_x + padded[0, :, 2:, 1:-1]) * scale
    c_west = 0.5 * (m_x + padded[0, :, :-2, 1:-1]) * scale
    c_north = 0.5 * (m_y + padded[1, :, 1:-1, 2:]) * scale
    c_south = 0.5 * (m_y + padded[1, :, 1:-1, :-2]) * scale
    c_upper = 0.5 * (m_z + jnp.roll(m_z, -1, 0)) * span_scale
    c_lower = 0.5 * (m_z + jnp.roll(m_z, 1, 0)) * span_scale
    c_diag = c_east + c_west + c_north + c_south + c_upper + c_lower
    return (c_east, c_west, c_north, c_south, c_upper, c_lower, c_diag)


def stencil(field, padded, coeffs):
    beside = coeffs[0] * padded[:, 2:, 1:-1] + coeffs[1] * padded[:, :-2, 1:-1]
    beside = beside + coeffs[2] * padded[:, 1:-1, 2:] + coeffs[3] * padded[:, 1:-1, :-2]
    beside = beside + coeffs[4] * jnp.roll(field, -1, 0) + coeffs[5] * jnp.roll(field, 1, 0)
    return coeffs[6] * field - beside


def local_apply(field, coeffs):
    padded = jnp.pad(field, ((0, 0), (1, 1), (1, 1)))
    return stencil(field, padded, coeffs)


def local_coeffs(metric, level_no):
    padded = jnp.pad(metric[:2], ((0, 0), (0, 0), (1, 1), (1, 1)))
    return face_coeffs(metric, padded, level_no)


def coarse_solve(source, coeffs):
    field = jnp.zeros_like(source)
    resid = source
    direction = source
    norm_now = jnp.sum(resid * resid)
    for sweep_no in range(CSWEEPS):
        image = local_apply(direction, coeffs)
        alpha = norm_now / jnp.sum(direction * image)
        field = field + alpha * direction
        resid = resid - alpha * image
        if sweep_no + 1 < CSWEEPS:
            norm_next = jnp.sum(resid * resid)
            direction = resid + (norm_next / norm_now) * direction
            norm_now = norm_next
    return field


def v_cycle(source, level_no, coeff_list):
    coeffs = coeff_list[level_no]
    if level_no == LEVELS - 1:
        return coarse_solve(source, coeffs)
    field = omega_relax * source / coeffs[6]
    field = field + omega_relax * (source - local_apply(field, coeffs)) / coeffs[6]
    remains = source - local_apply(field, coeffs)
    field = field + refine(v_cycle(coarsen(remains), level_no + 1, coeff_list))
    for sweep_no in range(2):
        field = field + omega_relax * (source - local_apply(field, coeffs)) / coeffs[6]
    return field


def reference(vorticity, metric):
    metrics = [metric]
    for level_no in range(1, LEVELS):
        metrics.append(coarsen(metrics[-1]))
    coeff_list = [local_coeffs(metrics[k], k) for k in range(LEVELS)]
    stream = v_cycle(vorticity, 0, coeff_list)
    residual = vorticity - local_apply(stream, coeff_list[0])
    return stream, residual
```

```python
import jax
import jax.numpy as jnp
from jax import lax
from jax.experimental import pallas as pl
from jax.experimental.pallas import tpu as pltpu
from jax.sharding import PartitionSpec as P

MESH = pl.DeviceIdType.MESH
NGX, NGY = 32, 8
OMEGA = 0.8
SPAN = 0.25**4
SWEEPS = 8
F32 = jnp.float32

LOW = (8, 4, 8, 4)
ROWS = (32, 16, 20, 10)


def lanes():
    return lax.broadcasted_iota(jnp.int32, (8, 128), 1)


def swap(x):
    return jnp.concatenate([x[:, 1:2], x[:, 0:1]], axis=1)


def north(x, step):
    turned = pltpu.roll(x, 128 - step, 3)
    return jnp.where(lanes() >= 128 - step, swap(turned), turned)


def south(x, step):
    turned = pltpu.roll(x, step, 3)
    return jnp.where(lanes() < step, swap(turned), turned)


def upper(x):
    return pltpu.roll(x, 7, x.ndim - 2)


def lower(x):
    return pltpu.roll(x, 1, x.ndim - 2)


def operate(v, cx, cy, cz, step):
    fx = cx * (v[:-1] - v[1:])
    mid = v[1:-1]
    fy = cy * (mid - north(mid, step))
    fz = cz * (mid - upper(mid))
    return (fx[1:] - fx[:-1]) + (fy - south(fy, step)) + (fz - lower(fz))


def pair_mean(total, step):
    axis = total.ndim - 1
    low = (lanes() // step) % 2 == 0
    other = jnp.where(low, pltpu.roll(total, 128 - step, axis), pltpu.roll(total, step, axis))
    return 0.25 * (total + other)


def coarsen(x, step):
    rows = x.shape[0]
    y = x.reshape((rows // 2, 2) + x.shape[1:])
    return pair_mean(y[:, 0] + y[:, 1], step)


def pick(x, index):
    return jnp.take_along_axis(x, index, axis=1)


def kernel(f_ref, m_ref, s_ref, q_ref,
           e0, kr, kl, rkl, rkr, rm2, rf2, ma, mb, fa, fb, rv3, rv1, v4, c4,
           f1, f2, f3, w0, w1, w2, w3, cx0, cx1, cx2, cx3, cy0, cy1, cy2, cy3, cz0, cz1, cz2, cz3,
           va0, va1, va2, va3, vb0, vb1, vb2, vb3,
           tiles, lines, ssem, r1_sem, recv):
    gx, gy = lax.axis_index("gx"), lax.axis_index("gy")
    xc, zc = gx // 8, gx % 8
    yc, cc = gy // 2, gy % 2
    CX, CY, CZ, W = (cx0, cx1, cx2, cx3), (cy0, cy1, cy2, cy3), (cz0, cz1, cz2, cz3), (w0, w1, w2, w3)
    VA, VB = (va0, va1, va2, va3), (vb0, vb1, vb2, vb3)
    lane = lanes()
    sub = lax.broadcasted_iota(jnp.int32, (8, 128), 0)

    def beside(dx, dy):
        return ((gx + dx + NGX) % NGX, (gy + dy + NGY) % NGY)

    wide = [(dx, dy) for dx in (-2, -1, 0, 1, 2) for dy in (-1, 0, 1) if (dx, dy) != (0, 0)]
    column = [(xc * 8 + (zc + dz) % 8, yc * 2 + (cc + dc) % 2) for dz in range(8) for dc in range(2) if (dz, dc) != (0, 0)]
    plane = [(((xc + dx) % 4) * 8 + zc, ((yc + dy) % 4) * 2 + cc) for dx in range(4) for dy in range(4) if (dx, dy) != (0, 0)]

    barrier = pltpu.get_barrier_semaphore()
    everyone = [beside(dx, dy) for dx, dy in wide] + column + plane
    for target in everyone:
        pl.semaphore_signal(barrier, inc=1, device_id=target, device_id_type=MESH)

    def send(src, dst, sem, to, out):
        copy = pltpu.make_async_remote_copy(
            src_ref=src, dst_ref=dst, send_sem=ssem.at[out], recv_sem=sem, device_id=to, device_id_type=MESH)
        copy.start()
        return copy

    def pieces(kind, count, sem):
        ref = kind.at[pl.ds(0, count)]
        pltpu.make_async_copy(ref, ref, sem).wait()

    for row in range(16):
        for arr in range(4):
            if arr == 1:
                tile = f_ref[pl.ds(row, 8, 16), :]
            else:
                tile = m_ref[pl.ds((arr - 1 if arr else 0) * 128 + row, 8, 16), :]
            e0[arr, 8 + row, 0] = tile
    for k in range(4):
        right, left = jnp.zeros((8, 128), F32), jnp.zeros((8, 128), F32)
        for g in range(16):
            turned = pltpu.roll(e0[g % 4, 8 + 4 * k + g // 4, 0], (8 * g + 8) % 128, 1)
            right = jnp.where(lane // 8 == g, turned, right)
            left = jnp.where(lane // 8 == (g + 1) % 16, turned, left)
        kr[k] = right
        kl[k] = left

    def spread_row(tile):
        turned = pick(tile, 16 * (lane % 8))
        return jnp.sum(jnp.where(sub == lane // 16, turned, 0.0), axis=0, keepdims=True)

    for comp in range(3):
        arr = (0, 2, 3)[comp]
        m1 = coarsen(e0[arr, 8:24, 0], 1)
        m2 = coarsen(m1, 2)
        m3 = coarsen(m2, 4)
        m4 = coarsen(m3, 8)
        part = lane % 4
        rm2[7, comp] = jnp.where(part == 0, m2[0], jnp.where(part == 1, m2[1], jnp.where(part == 2, m2[2], m2[3])))
        ma[cc, comp, pl.ds(zc, 1)] = spread_row(m4[0])

    pl.semaphore_wait(barrier, len(everyone))

    sends = []
    east, west = beside(1, 0), beside(-1, 0)
    rest = pl.ds(1, 3)
    sends.append(send(e0.at[0, pl.ds(16, 8), 0], e0.at[0, pl.ds(0, 8), 0], r1_sem.at[0], east, 0))
    sends.append(send(e0.at[0, pl.ds(8, 8), 0], e0.at[0, pl.ds(24, 8), 0], r1_sem.at[1], west, 1))
    sends.append(send(e0.at[rest, pl.ds(18, 6), 0], e0.at[rest, pl.ds(2, 6), 0], r1_sem.at[2], east, 2))
    sends.append(send(e0.at[rest, pl.ds(8, 6), 0], e0.at[rest, pl.ds(24, 6), 0], r1_sem.at[3], west, 3))
    for side, (packed, into) in enumerate(((kr, rkl), (kl, rkr))):
        dy = 1 - 2 * side
        for n, (dx, a, b, c) in enumerate(((1, 2, 2, 0), (-1, 0, 2, 6), (0, 0, 4, 2))):
            slot = 4 + 3 * side + n
            sends.append(send(packed.at[pl.ds(a, b)], into.at[pl.ds(c, b)], r1_sem.at[slot], beside(dx, dy), slot))
    for dx, dy in wide:
        send(rm2.at[7], rm2.at[7 - dx * 3 - dy], recv.at[0], beside(dx, dy), 10)
    for target in column:
        mine = ma.at[cc, pl.ds(0, 3), pl.ds(zc, 1)]
        send(mine, mine, recv.at[1], target, 11)
    for copy in sends:
        copy.wait_recv()

    even = (lane // 8) % 2 == 0
    for k in range(8):
        me = jnp.where(even, rkl[k], rkr[k])
        mo = jnp.where(even, rkr[k], rkl[k])
        for g in range(16):
            e0[g % 4, 4 * k + g // 4, 1] = pltpu.roll(me if g % 2 == 0 else mo, (120 - 8 * g) % 128, 1)

    has_left, has_right = gy > 0, gy < NGY - 1

    def side_mask(reach):
        inside = jnp.logical_or(jnp.logical_and(lane < reach, has_right), jnp.logical_and(lane >= 128 - reach, has_left))
        return inside.astype(F32)

    mask0, mask2 = side_mask(8), side_mask(64)

    def row_inside(level, row):
        own = 16 >> level
        if row < 0:
            need = -(row // own)
            return (gx >= need).astype(F32)
        if row >= own:
            return (gx + row // own <= NGX - 1).astype(F32)
        return None

    def masked(tile, level, row, part):
        side = mask0 if level < 2 else mask2
        scale = row_inside(level, row)
        if part == 1:
            tile = tile * side
        return tile if scale is None else tile * scale

    for arr in (0, 2, 3):
        for row in range(-8 if arr == 0 else -6, 24 if arr == 0 else 22):
            for part in range(2):
                if part == 1 or row < 0 or row >= 16:
                    e0[arr, row + 8, part] = masked(e0[arr, row + 8, part], 0, row, part)

    def coefficients(level, mx, my, mz, lo, hi):
        low, step = LOW[level], 1 << level
        half, spans = 0.5 * 0.25**level, 0.5 * SPAN
        for a in range(lo, hi, 4):
            b = min(a + 4, hi)
            x = mx(a - 1, b + 1)
            cx = half * (x[:-1] + x[1:])
            y = my(a, b)
            cy = half * (y + north(y, step))
            z = mz(a, b)
            cz = spans * (z + upper(z))
            CX[level][a - 1 + low:b + low] = cx
            CY[level][a + low:b + low] = cy
            CZ[level][a + low:b + low] = cz
            diag = cx[:-1] + cx[1:] + cy + south(cy, step) + cz + lower(cz)
            w = OMEGA / diag
            for row in range(a, b):
                for part in range(2):
                    tile = w[row - a, part]
                    side = mask0 if level < 2 else mask2
                    scale = row_inside(level, row)
                    if part == 1:
                        tile = jnp.where(side > 0, tile, 0.0)
                    if scale is not None:
                        tile = jnp.where(scale > 0, tile, 0.0)
                    W[level][row + low, part] = tile

    def field(level, source, target, lo, hi, f_of, relax, chunk=4):
        low, step = LOW[level], 1 << level
        for a in range(lo, hi, chunk):
            b = min(a + chunk, hi)
            v = source[a - 1 + low:b + 1 + low]
            left = f_of(a, b) - operate(
                v, CX[level][a - 1 + low:b + low], CY[level][a + low:b + low], CZ[level][a + low:b + low], step)
            target(a, b, v[1:-1] + W[level][a + low:b + low] * left if relax else left)

    def into(ref, level):
        def store(a, b, value):
            ref[a + LOW[level]:b + LOW[level]] = value
        return store

    def into_coarse(ref, level):
        def store(a, b, value):
            ref[a // 2 + LOW[level + 1]:b // 2 + LOW[level + 1]] = coarsen(value, 1 << level)
        return store

    def rows_of(ref, level):
        return lambda a, b: ref[a + LOW[level]:b + LOW[level]]

    def start(level, f_of, lo, hi):
        low = LOW[level]
        for a in range(lo, hi, 4):
            b = min(a + 4, hi)
            VA[level][a + low:b + low] = W[level][a + low:b + low] * f_of(a, b)

    def arr0(arr):
        return lambda a, b: e0[arr, a + 8:b + 8]

    coefficients(0, arr0(0), arr0(2), arr0(3), -6, 22)
    start(0, arr0(1), -6, 22)
    field(0, va0, into(vb0, 0), -5, 21, arr0(1), True)
    field(0, vb0, into_coarse(f1, 0), -4, 20, arr0(1), False)

    def coarse0(arr):
        return lambda a, b: coarsen(e0[arr, 2 * a + 8:2 * b + 8], 1)

    coefficients(1, coarse0(0), coarse0(2), coarse0(3), -3, 11)
    start(1, rows_of(f1, 1), -2, 10)
    field(1, va1, into(vb1, 1), -1, 9, rows_of(f1, 1), True)
    own2 = []

    def keep(a, b, value):
        own2.append(coarsen(value[:, 0], 2))

    field(1, vb1, keep, 0, 8, rows_of(f1, 1), False)
    part = lane % 4
    rf2[7] = jnp.where(part == 0, own2[0][0], jnp.where(part == 1, own2[0][1], jnp.where(part == 2, own2[1][0], own2[1][1])))
    for dx, dy in wide:
        send(rf2.at[7], rf2.at[7 - dx * 3 - dy], recv.at[2], beside(dx, dy), 12)

    pieces(tiles, 42, recv.at[0])
    pieces(lines, 45, recv.at[1])
    own4 = [jnp.where((lane // 8) % 2 == 0, ma[0, comp], ma[1, comp]) for comp in range(3)]
    for comp in range(3):
        mb[xc, yc, comp] = own4[comp]
    for target in plane:
        send(mb.at[xc, yc], mb.at[xc, yc], recv.at[3], target, 13)

    quads = [(lane // 4) * 4 + j for j in range(4)]

    def rows2(of, a, b):
        out = []
        for row in range(a, b):
            block = (row // 4 + 2) * 3
            main = of(block + 1)
            side = jnp.where(lane < 64, of(block + 2), of(block))
            out.append(jnp.stack([pick(main, quads[row % 4]), pick(side, quads[row % 4])]))
        return jnp.stack(out)

    def metric2(comp):
        def rows(a, b):
            got = rows2(lambda slot: rm2[slot, comp], a, b)
            return jnp.stack([jnp.stack([masked(got[n, p], 2, a + n, p) for p in range(2)]) for n in range(b - a)])
        return rows

    def metric3(comp):
        return lambda a, b: coarsen(metric2(comp)(2 * a, 2 * b), 4)

    coefficients(2, metric2(0), metric2(1), metric2(2), -7, 11)
    coefficients(3, metric3(0), metric3(1), metric3(2), -3, 5)

    pieces(tiles, 14, recv.at[2])
    for a in range(-6, 10, 4):
        f2[a + 8:a + 12] = rows2(lambda slot: rf2[slot], a, a + 4)
    start(2, rows_of(f2, 2), -6, 10)
    field(2, va2, into(vb2, 2), -5, 9, rows_of(f2, 2), True)
    field(2, vb2, into_coarse(f3, 2), -4, 8, rows_of(f2, 2), False)
    start(3, rows_of(f3, 3), -2, 4)
    field(3, va3, into(vb3, 3), -1, 3, rows_of(f3, 3), True)
    own4f = []

    def keep4(a, b, value):
        own4f.append(coarsen(value[:, 0], 8))

    field(3, vb3, keep4, 0, 2, rows_of(f3, 3), False)
    fa[cc, pl.ds(zc, 1)] = spread_row(own4f[0][0])
    for target in column:
        mine = fa.at[cc, pl.ds(zc, 1)]
        send(mine, mine, recv.at[4], target, 14)

    pieces(tiles, 45, recv.at[3])
    lane16 = lane % 16
    four = 0.5 * 0.25**4

    def next_x(v):
        turned = upper(v)
        return jnp.where(sub == 7, jnp.concatenate([turned[1:], turned[:1]], axis=0), turned)

    def last_x(v):
        turned = lower(v)
        return jnp.where(sub == 0, jnp.concatenate([turned[3:], turned[:3]], axis=0), turned)

    def next_y(v):
        far = pltpu.roll(v, 15, 3)
        return jnp.where(lane16 == 15, jnp.concatenate([far[:, 1:], far[:, :1]], axis=1), pltpu.roll(v, 127, 3))

    def last_y(v):
        far = pltpu.roll(v, 113, 3)
        return jnp.where(lane16 == 0, jnp.concatenate([far[:, 3:], far[:, :3]], axis=1), pltpu.roll(v, 1, 3))

    def next_z(v):
        return pltpu.roll(v, 112, 3)

    def last_z(v):
        return pltpu.roll(v, 16, 3)

    def blank(x, axis, where, cond):
        pieces = []
        for n in range(4):
            piece = lax.slice_in_dim(x, n, n + 1, axis=axis)
            pieces.append(jnp.where(cond, 0.0, piece) if n == where else piece)
        return jnp.concatenate(pieces, axis=axis)

    mx, my, mz = mb[:, :, 0], mb[:, :, 1], mb[:, :, 2]
    mxe, mxw = blank(next_x(mx), 0, 3, sub == 7), blank(last_x(mx), 0, 0, sub == 0)
    myn, mys = blank(next_y(my), 1, 3, lane16 == 15), blank(last_y(my), 1, 0, lane16 == 0)
    ce, cw, cn, cs = four * (mx + mxe), four * (mx + mxw), four * (my + myn), four * (my + mys)
    cu, cl = four * (mz + next_z(mz)), four * (mz + last_z(mz))
    c4[6] = ce + cw + cn + cs + cu + cl
    c4[0] = blank(ce, 0, 3, sub == 7)
    c4[1] = blank(cw, 0, 0, sub == 0)
    c4[2] = blank(cn, 1, 3, lane16 == 15)
    c4[3] = blank(cs, 1, 0, lane16 == 0)
    c4[4] = cu
    c4[5] = cl

    pieces(lines, 15, recv.at[4])
    fb[xc, yc] = jnp.where((lane // 8) % 2 == 0, fa[0], fa[1])
    for target in plane:
        send(fb.at[xc, yc], fb.at[xc, yc], recv.at[5], target, 15)

    rv3[7] = jnp.where(part == 0, vb3[4, 0], jnp.where(part == 1, vb3[5, 0], jnp.where(part == 2, f3[4, 0], f3[5, 0])))
    for dx, dy in wide:
        send(rv3.at[7], rv3.at[7 - dx * 3 - dy], recv.at[6], beside(dx, dy), 16)
    for row in range(8):
        rv1[1, 4 + row] = jnp.where(lane % 2 == 0, vb1[4 + row, 0], f1[4 + row, 0])
    for dx in (-1, 0, 1):
        for dy in (-1, 0, 1):
            if (dx, dy) != (0, 0):
                a, b, c = ((4, 4, 12), (4, 8, 4), (8, 4, 0))[dx + 1]
                send(rv1.at[1, pl.ds(a, b)], rv1.at[1 - dy, pl.ds(c, b)], recv.at[7], beside(dx, dy), 17)

    pieces(tiles, 15, recv.at[5])

    def total(x):
        tile = jnp.sum(x, axis=(0, 1))
        return jnp.sum(jnp.sum(tile, axis=0, keepdims=True), axis=1, keepdims=True)

    def image_of(p):
        out = c4[6] * p - c4[0] * next_x(p) - c4[1] * last_x(p)
        out = out - c4[2] * next_y(p) - c4[3] * last_y(p)
        return out - c4[4] * next_z(p) - c4[5] * last_z(p)

    r = fb[...]
    p = r
    v = jnp.zeros_like(r)
    rr = total(r * r)
    for sweep in range(SWEEPS):
        q = image_of(p)
        alpha = rr / total(p * q)
        v = v + alpha * p
        if sweep + 1 < SWEEPS:
            r = r - alpha * q
            new = total(r * r)
            p = r + (new / rr) * p
            rr = new
    v4[...] = v

    main_index = sub * 16 + cc * 8 + lane // 16
    side_index = sub * 16 + (cc * 8 + 8 + lane // 16) % 16
    other_y = jnp.clip(yc + 2 * cc - 1, 0, 3)
    near = jnp.logical_xor(lane < 64, cc == 1)
    pieces(tiles, 14, recv.at[6])
    octs = [(lane // 8) * 8 + j for j in range(4)]
    for d in range(-2, 3):
        x = jnp.clip(gx + d, 0, NGX - 1)
        here = jnp.broadcast_to(v4[x // 8, yc, pl.ds(x % 8, 1)], (8, 128))
        there = jnp.broadcast_to(v4[x // 8, other_y, pl.ds(x % 8, 1)], (8, 128))
        main = pick(here, main_index)
        side = jnp.where(near, pick(here, side_index), pick(there, side_index)) * mask2
        block = (d + 2) * 3
        packed = (rv3[block + 1], jnp.where(lane < 64, rv3[block + 2], rv3[block]))
        inside = row_inside(3, 2 * d)
        for j in range(2):
            row = 2 * d + j
            for p_no in range(2):
                value = pick(packed[p_no], octs[j])
                if p_no == 1:
                    value = value * mask2
                value = value + (main if p_no == 0 else side)
                va3[row + 4, p_no] = value if inside is None else value * inside
                if -3 <= row < 5:
                    f3[row + 4, p_no] = pick(packed[p_no], octs[2 + j])
    field(3, va3, into(vb3, 3), -3, 5, rows_of(f3, 3), True)
    field(3, vb3, into(va3, 3), -2, 4, rows_of(f3, 3), True)

    def refined(ref, level, a, b):
        x = ref[a + LOW[level]:b + LOW[level]]
        return jnp.stack([x, x], axis=1).reshape((2 * (b - a),) + x.shape[1:])

    def correct(level, a, b):
        low = LOW[level]
        for n in range(a, b, 4):
            m = min(n + 4, b)
            VA[level][n + low:m + low] = VB[level][n + low:m + low] + refined(VA[level + 1], level + 1, n // 2, m // 2)

    correct(2, -4, 8)
    field(2, va2, into(vb2, 2), -3, 7, rows_of(f2, 2), True)
    field(2, vb2, into(va2, 2), -2, 6, rows_of(f2, 2), True)

    pieces(tiles, 40, recv.at[7])
    evens, odds = (lane // 2) * 2, (lane // 2) * 2 + 1
    for row in range(-4, 12):
        inside = row_inside(1, row)
        if inside is not None:
            value = pick(rv1[1, row + 4], evens)
            vb1[row + 4, 0] = value * inside
            f1[row + 4, 0] = pick(rv1[1, row + 4], odds)
        packed = jnp.where(lane < 64, rv1[2, row + 4], rv1[0, row + 4])
        value = pick(packed, evens) * mask0
        vb1[row + 4, 1] = value if inside is None else value * inside
        f1[row + 4, 1] = pick(packed, odds)
    correct(1, -4, 12)
    field(1, va1, into(vb1, 1), -3, 11, rows_of(f1, 1), True)
    field(1, vb1, into(va1, 1), -2, 10, rows_of(f1, 1), True)

    for a in range(-2, 9):
        lo = -3 if a == -2 else 2 * a
        hi = 2 * a + 2
        add = va1[a + 4]
        for row in range(lo, hi):
            va0[row + 8] = vb0[row + 8] + add
    va0[18 + 8] = vb0[18 + 8] + va1[9 + 4]
    field(0, va0, into(vb0, 0), -2, 18, arr0(1), True)

    def out_stream(a, b, value):
        va0[a + 8:b + 8] = value
        for row in range(max(a, 0), min(b, 16)):
            s_ref[pl.ds(row, 8, 16), :] = value[row - a, 0]

    def out_residual(a, b, value):
        for row in range(a, b):
            q_ref[pl.ds(row, 8, 16), :] = value[row - a, 0]

    field(0, vb0, out_stream, -1, 17, arr0(1), True)
    field(0, va0, out_residual, 0, 16, arr0(1), False)

    for copy in sends:
        copy.wait_send()
    for group, (kind, count) in enumerate(
            ((tiles, 42), (lines, 45), (tiles, 14), (tiles, 45), (lines, 15), (tiles, 15), (tiles, 14), (tiles, 40))):
        pieces(kind, count, ssem.at[10 + group])


def level_scratch():
    shapes = []
    for level in range(4):
        shapes.append(pltpu.VMEM((ROWS[level], 2, 8, 128), F32))
    return shapes


def on_device(vorticity, metric):
    depth, rows, columns = vorticity.shape
    tile = (8, 128)
    scratch = [
        pltpu.VMEM((4, 32, 2) + tile, F32),
        pltpu.VMEM((4,) + tile, F32), pltpu.VMEM((4,) + tile, F32),
        pltpu.VMEM((8,) + tile, F32), pltpu.VMEM((8,) + tile, F32),
        pltpu.VMEM((15, 3) + tile, F32), pltpu.VMEM((15,) + tile, F32),
        pltpu.VMEM((2, 3) + tile, F32), pltpu.VMEM((4, 4, 3) + tile, F32),
        pltpu.VMEM((2,) + tile, F32), pltpu.VMEM((4, 4) + tile, F32),
        pltpu.VMEM((15,) + tile, F32), pltpu.VMEM((3, 16) + tile, F32),
        pltpu.VMEM((4, 4) + tile, F32), pltpu.VMEM((7, 4, 4) + tile, F32),
    ]
    scratch += level_scratch()[1:]
    for _ in range(6):
        scratch += level_scratch()
    scratch += [pltpu.VMEM((45,) + tile, F32), pltpu.VMEM((45, 1, 128), F32)]
    scratch += [pltpu.SemaphoreType.DMA((18,)), pltpu.SemaphoreType.DMA((10,)), pltpu.SemaphoreType.DMA((8,))]
    flat = jax.ShapeDtypeStruct((depth * rows, columns), F32)
    vmem = pl.BlockSpec(memory_space=pltpu.VMEM)
    stream, residual = pl.pallas_call(
        kernel,
        out_shape=(flat, flat),
        in_specs=[vmem, vmem],
        out_specs=(vmem, vmem),
        scratch_shapes=scratch,
        compiler_params=pltpu.CompilerParams(collective_id=0, has_side_effects=True, vmem_limit_bytes=48 * 1024 * 1024),
    )(vorticity.reshape(depth * rows, columns), metric.reshape(3 * depth * rows, columns))
    return stream.reshape(vorticity.shape), residual.reshape(vorticity.shape)


def solution(mesh):
    return jax.shard_map(
        on_device,
        mesh=mesh,
        in_specs=(P(None, "gx", "gy"), P(None, None, "gx", "gy")),
        out_specs=(P(None, "gx", "gy"), P(None, "gx", "gy")),
        check_vma=False,
    )
```

```python
import jax
import jax.numpy as jnp
from jax import lax
from jax.experimental import pallas as pl
from jax.experimental.pallas import tpu as pltpu
from jax.sharding import PartitionSpec as P

MESH = pl.DeviceIdType.MESH
NGX, NGY = 32, 8
OMEGA = 0.8
SPAN = 0.25**4
SWEEPS = 8
F32 = jnp.float32

LOW = (8, 4, 8, 4)
ROWS = (32, 16, 20, 10)


def lanes():
    return lax.broadcasted_iota(jnp.int32, (8, 128), 1)


def swap(x):
    return jnp.concatenate([x[:, 1:2], x[:, 0:1]], axis=1)


def north(x, step):
    turned = pltpu.roll(x, 128 - step, 3)
    return jnp.where(lanes() >= 128 - step, swap(turned), turned)


def south(x, step):
    turned = pltpu.roll(x, step, 3)
    return jnp.where(lanes() < step, swap(turned), turned)


def upper(x):
    return pltpu.roll(x, 7, x.ndim - 2)


def lower(x):
    return pltpu.roll(x, 1, x.ndim - 2)


def operate(v, cx, cy, cz, step):
    fx = cx * (v[:-1] - v[1:])
    mid = v[1:-1]
    fy = cy * (mid - north(mid, step))
    fz = cz * (mid - upper(mid))
    return (fx[1:] - fx[:-1]) + (fy - south(fy, step)) + (fz - lower(fz))


def coarsen_field(x, step):
    y = x.reshape((x.shape[0] // 2, 2) + x.shape[1:])
    both, axis = y[:, 0] + y[:, 1], x.ndim - 1
    other = jnp.where((lanes() & step) == 0, pltpu.roll(both, 128 - step, axis), pltpu.roll(both, step, axis))
    return 0.25 * (both + other)


def moved(x, matrix):
    first = x.astype(jnp.bfloat16)
    rest = x - first.astype(F32)
    second = rest.astype(jnp.bfloat16)
    third = (rest - second.astype(F32)).astype(jnp.bfloat16)
    terms = [jnp.dot(term, matrix, preferred_element_type=F32) for term in (first, second, third)]
    return terms[0] + (terms[1] + terms[2])


def pick(x, index):
    return jnp.take_along_axis(x, index, axis=1)


def kernel(f_ref, m_ref, s_ref, q_ref,
           e0, m1, pairs, f_in, m_in, in_sem, kr, kl, rkl, rkr, rm2, rf2, ma, mb, fa, fb, rv3, rv1, v4, c4,
           f1, f2, f3, w0, w1, w2, w3, cx0, cx1, cx2, cx3, cy0, cy1, cy2, cy3, cz0, cz1, cz2, cz3,
           va0, va1, va2, va3, vb0, vb1, vb2, vb3,
           tiles, lines, ssem, r1_sem, recv):
    gx, gy = lax.axis_index("gx"), lax.axis_index("gy")
    xc, zc = gx >> 3, gx & 7
    yc, cc = gy >> 1, gy & 1
    CX, CY, CZ, W = (cx0, cx1, cx2, cx3), (cy0, cy1, cy2, cy3), (cz0, cz1, cz2, cz3), (w0, w1, w2, w3)
    VA, VB = (va0, va1, va2, va3), (vb0, vb1, vb2, vb3)
    lane = lanes()
    sub = lax.broadcasted_iota(jnp.int32, (8, 128), 0)
    slot = lane >> 3

    def beside(dx, dy):
        return ((gx + dx + NGX) % NGX, (gy + dy + NGY) % NGY)

    wide = [(dx, dy) for dx in (-2, -1, 0, 1, 2) for dy in (-1, 0, 1) if (dx, dy) != (0, 0)]
    column = [(xc * 8 + (zc + dz) % 8, yc * 2 + (cc + dc) % 2) for dz in range(8) for dc in range(2) if (dz, dc) != (0, 0)]
    plane = [(((xc + dx) % 4) * 8 + zc, ((yc + dy) % 4) * 2 + cc) for dx in range(4) for dy in range(4) if (dx, dy) != (0, 0)]

    def pair_mean(total, step):
        return moved(total.reshape(-1, 128), pairs[step.bit_length() - 1]).reshape(total.shape)

    def coarsen(x, step):
        y = x.reshape((x.shape[0] // 2, 2) + x.shape[1:])
        return pair_mean(y[:, 0] + y[:, 1], step)

    barrier = pltpu.get_barrier_semaphore()
    everyone = [beside(dx, dy) for dx, dy in wide] + column + plane
    for target in everyone:
        pl.semaphore_signal(barrier, inc=1, device_id=target, device_id_type=MESH)

    def send(src, dst, sem, to, out):
        copy = pltpu.make_async_remote_copy(
            src_ref=src, dst_ref=dst, send_sem=ssem.at[out], recv_sem=sem, device_id=to, device_id_type=MESH)
        copy.start()
        return copy

    def pieces(kind, count, sem):
        ref = kind.at[pl.ds(0, count)]
        pltpu.make_async_copy(ref, ref, sem).wait()

    source = lax.broadcasted_iota(jnp.int32, (128, 128), 0)
    goal = lax.broadcasted_iota(jnp.int32, (128, 128), 1)

    def matrix_of(condition, value=1.0):
        return jnp.where(condition, value, 0.0).astype(jnp.bfloat16)

    loads = [pltpu.make_async_copy(m_ref, m_in, in_sem.at[0]), pltpu.make_async_copy(f_ref, f_in, in_sem.at[1])]
    for copy in loads:
        copy.start()
    for copy in loads:
        copy.wait()

    for row in range(16):
        for arr in range(4):
            if arr == 1:
                tile = f_in[pl.ds(row, 8, 16), :]
            else:
                tile = m_in[pl.ds((arr - 1 if arr else 0) * 128 + row, 8, 16), :]
            e0[arr, 8 + row, 0] = tile
    for k in range(4):
        right, left = jnp.zeros((8, 128), F32), jnp.zeros((8, 128), F32)
        for g in range(16):
            turned = pltpu.roll(e0[g % 4, 8 + 4 * k + g // 4, 0], (8 * g + 8) % 128, 1)
            right = jnp.where(slot == g, turned, right)
            left = jnp.where(slot == (g + 1) % 16, turned, left)
        kr[k] = right
        kl[k] = left

    def spread_row(tile):
        turned = pick(tile, 16 * (lane & 7))
        return jnp.sum(jnp.where(sub == (lane >> 4), turned, 0.0), axis=0, keepdims=True)

    pl.semaphore_wait(barrier, len(everyone))

    sends = []
    east, west = beside(1, 0), beside(-1, 0)
    rest = pl.ds(1, 3)
    sends.append(send(e0.at[0, pl.ds(16, 8), 0], e0.at[0, pl.ds(0, 8), 0], r1_sem.at[0], east, 0))
    sends.append(send(e0.at[0, pl.ds(8, 8), 0], e0.at[0, pl.ds(24, 8), 0], r1_sem.at[1], west, 1))
    sends.append(send(e0.at[rest, pl.ds(18, 6), 0], e0.at[rest, pl.ds(2, 6), 0], r1_sem.at[2], east, 2))
    sends.append(send(e0.at[rest, pl.ds(8, 6), 0], e0.at[rest, pl.ds(24, 6), 0], r1_sem.at[3], west, 3))
    for side, (packed, into) in enumerate(((kr, rkl), (kl, rkr))):
        dy = 1 - 2 * side
        for n, (dx, a, b, c) in enumerate(((1, 2, 2, 0), (-1, 0, 2, 6), (0, 0, 4, 2))):
            at = 4 + 3 * side + n
            sends.append(send(packed.at[pl.ds(a, b)], into.at[pl.ds(c, b)], r1_sem.at[at], beside(dx, dy), at))
    for n in range(4):
        pairs[n] = matrix_of(jnp.logical_or(source == goal, source == (goal ^ (1 << n))), 0.25)
    for comp in range(3):
        arr = (0, 2, 3)[comp]
        m2 = coarsen(coarsen(e0[arr, 8:24, 0], 1), 2)
        m3 = coarsen(m2, 4)
        m4 = coarsen(m3, 8)
        part = lane & 3
        rm2[7, comp] = jnp.where(part == 0, m2[0], jnp.where(part == 1, m2[1], jnp.where(part == 2, m2[2], m2[3])))
        ma[cc, comp, pl.ds(zc, 1)] = spread_row(m4[0])

    for dx, dy in wide:
        send(rm2.at[7], rm2.at[7 - dx * 3 - dy], recv.at[0], beside(dx, dy), 10)
    for target in column:
        mine = ma.at[cc, pl.ds(0, 3), pl.ds(zc, 1)]
        send(mine, mine, recv.at[1], target, 11)
    for copy in sends:
        copy.wait_recv()

    even = (lane & 8) == 0
    for k in range(8):
        me = jnp.where(even, rkl[k], rkr[k])
        mo = jnp.where(even, rkr[k], rkl[k])
        for g in range(16):
            e0[g % 4, 4 * k + g // 4, 1] = pltpu.roll(me if g % 2 == 0 else mo, (120 - 8 * g) % 128, 1)

    has_left, has_right = gy > 0, gy < NGY - 1

    def side_mask(reach):
        inside = jnp.logical_or(jnp.logical_and(lane < reach, has_right), jnp.logical_and(lane >= 128 - reach, has_left))
        return inside.astype(F32)

    mask0, mask2 = side_mask(8), side_mask(64)

    def row_inside(level, row):
        own = 16 >> level
        if row < 0:
            need = -(row // own)
            return (gx >= need).astype(F32)
        if row >= own:
            return (gx + row // own <= NGX - 1).astype(F32)
        return None

    def masked(tile, level, row, part):
        side = mask0 if level < 2 else mask2
        scale = row_inside(level, row)
        if part == 1:
            tile = tile * side
        return tile if scale is None else tile * scale

    for arr in (0, 2, 3):
        for row in range(-8 if arr == 0 else -6, 24 if arr == 0 else 22):
            for part in range(2):
                if part == 1 or row < 0 or row >= 16:
                    e0[arr, row + 8, part] = masked(e0[arr, row + 8, part], 0, row, part)

    def coefficients(level, mx, my, mz, lo, hi):
        low, step = LOW[level], 1 << level
        half, spans = 0.5 * 0.25**level, 0.5 * SPAN
        for a in range(lo, hi, 4):
            b = min(a + 4, hi)
            x = mx(a - 1, b + 1)
            cx = half * (x[:-1] + x[1:])
            y = my(a, b)
            cy = half * (y + north(y, step))
            z = mz(a, b)
            cz = spans * (z + upper(z))
            CX[level][a - 1 + low:b + low] = cx
            CY[level][a + low:b + low] = cy
            CZ[level][a + low:b + low] = cz
            diag = cx[:-1] + cx[1:] + cy + south(cy, step) + cz + lower(cz)
            w = OMEGA / diag
            for row in range(a, b):
                for part in range(2):
                    tile = w[row - a, part]
                    side = mask0 if level < 2 else mask2
                    scale = row_inside(level, row)
                    if part == 1:
                        tile = jnp.where(side > 0, tile, 0.0)
                    if scale is not None:
                        tile = jnp.where(scale > 0, tile, 0.0)
                    W[level][row + low, part] = tile

    def field(level, source, target, lo, hi, f_of, relax, chunk=4):
        low, step = LOW[level], 1 << level
        for a in range(lo, hi, chunk):
            b = min(a + chunk, hi)
            v = source[a - 1 + low:b + 1 + low]
            left = f_of(a, b) - operate(
                v, CX[level][a - 1 + low:b + low], CY[level][a + low:b + low], CZ[level][a + low:b + low], step)
            target(a, b, v[1:-1] + W[level][a + low:b + low] * left if relax else left)

    def into(ref, level):
        def store(a, b, value):
            ref[a + LOW[level]:b + LOW[level]] = value
        return store

    def into_coarse(ref, level):
        def store(a, b, value):
            ref[a // 2 + LOW[level + 1]:b // 2 + LOW[level + 1]] = coarsen_field(value, 1 << level)
        return store

    def rows_of(ref, level):
        return lambda a, b: ref[a + LOW[level]:b + LOW[level]]

    def start(level, f_of, lo, hi):
        low = LOW[level]
        for a in range(lo, hi, 4):
            b = min(a + 4, hi)
            VA[level][a + low:b + low] = W[level][a + low:b + low] * f_of(a, b)

    def arr0(arr):
        return lambda a, b: e0[arr, a + 8:b + 8]

    coefficients(0, arr0(0), arr0(2), arr0(3), -6, 22)
    start(0, arr0(1), -6, 22)
    field(0, va0, into(vb0, 0), -5, 21, arr0(1), True)
    field(0, vb0, into_coarse(f1, 0), -4, 20, arr0(1), False)

    for comp, arr in enumerate((0, 2, 3)):
        lo, hi = (-4, 12) if arr == 0 else (-3, 11)
        m1[comp, lo + 4:hi + 4] = coarsen(e0[arr, 2 * lo + 8:2 * hi + 8], 1)

    def coarse1(comp):
        return lambda a, b: m1[comp, a + 4:b + 4]

    coefficients(1, coarse1(0), coarse1(1), coarse1(2), -3, 11)
    start(1, rows_of(f1, 1), -2, 10)
    field(1, va1, into(vb1, 1), -1, 9, rows_of(f1, 1), True)
    own2 = []

    def keep(a, b, value):
        own2.append(coarsen_field(value[:, 0], 2))

    field(1, vb1, keep, 0, 8, rows_of(f1, 1), False)
    part = lane & 3
    rf2[7] = jnp.where(part == 0, own2[0][0], jnp.where(part == 1, own2[0][1], jnp.where(part == 2, own2[1][0], own2[1][1])))
    for dx, dy in wide:
        send(rf2.at[7], rf2.at[7 - dx * 3 - dy], recv.at[2], beside(dx, dy), 12)

    pieces(tiles, 42, recv.at[0])
    pieces(lines, 45, recv.at[1])
    own4 = [jnp.where((lane & 8) == 0, ma[0, comp], ma[1, comp]) for comp in range(3)]
    for comp in range(3):
        mb[xc, yc, comp] = own4[comp]
    for target in plane:
        send(mb.at[xc, yc], mb.at[xc, yc], recv.at[3], target, 13)

    quads = [(lane & ~3) + j for j in range(4)]

    def rows2(of, a, b):
        out = []
        for row in range(a, b):
            block = (row // 4 + 2) * 3
            main = of(block + 1)
            side = jnp.where(lane < 64, of(block + 2), of(block))
            out.append(jnp.stack([pick(main, quads[row % 4]), pick(side, quads[row % 4])]))
        return jnp.stack(out)

    def metric2(comp):
        def rows(a, b):
            got = rows2(lambda slot: rm2[slot, comp], a, b)
            return jnp.stack([jnp.stack([masked(got[n, p], 2, a + n, p) for p in range(2)]) for n in range(b - a)])
        return rows

    def metric3(comp):
        return lambda a, b: coarsen(metric2(comp)(2 * a, 2 * b), 4)

    coefficients(2, metric2(0), metric2(1), metric2(2), -7, 11)
    coefficients(3, metric3(0), metric3(1), metric3(2), -3, 5)

    pieces(tiles, 14, recv.at[2])
    for a in range(-6, 10, 4):
        f2[a + 8:a + 12] = rows2(lambda slot: rf2[slot], a, a + 4)
    start(2, rows_of(f2, 2), -6, 10)
    field(2, va2, into(vb2, 2), -5, 9, rows_of(f2, 2), True)
    field(2, vb2, into_coarse(f3, 2), -4, 8, rows_of(f2, 2), False)
    start(3, rows_of(f3, 3), -2, 4)
    field(3, va3, into(vb3, 3), -1, 3, rows_of(f3, 3), True)
    own4f = []

    def keep4(a, b, value):
        own4f.append(coarsen_field(value[:, 0], 8))

    field(3, vb3, keep4, 0, 2, rows_of(f3, 3), False)
    fa[cc, pl.ds(zc, 1)] = spread_row(own4f[0][0])
    for target in column:
        mine = fa.at[cc, pl.ds(zc, 1)]
        send(mine, mine, recv.at[4], target, 14)

    pieces(tiles, 45, recv.at[3])
    lane16 = lane & 15
    four = 0.5 * 0.25**4

    def next_x(v):
        turned = upper(v)
        return jnp.where(sub == 7, jnp.concatenate([turned[1:], turned[:1]], axis=0), turned)

    def last_x(v):
        turned = lower(v)
        return jnp.where(sub == 0, jnp.concatenate([turned[3:], turned[:3]], axis=0), turned)

    def next_y(v):
        far = pltpu.roll(v, 15, 3)
        return jnp.where(lane16 == 15, jnp.concatenate([far[:, 1:], far[:, :1]], axis=1), pltpu.roll(v, 127, 3))

    def last_y(v):
        far = pltpu.roll(v, 113, 3)
        return jnp.where(lane16 == 0, jnp.concatenate([far[:, 3:], far[:, :3]], axis=1), pltpu.roll(v, 1, 3))

    def next_z(v):
        return pltpu.roll(v, 112, 3)

    def last_z(v):
        return pltpu.roll(v, 16, 3)

    def blank(x, axis, where, cond):
        pieces = []
        for n in range(4):
            piece = lax.slice_in_dim(x, n, n + 1, axis=axis)
            pieces.append(jnp.where(cond, 0.0, piece) if n == where else piece)
        return jnp.concatenate(pieces, axis=axis)

    mx, my, mz = mb[:, :, 0], mb[:, :, 1], mb[:, :, 2]
    mxe, mxw = blank(next_x(mx), 0, 3, sub == 7), blank(last_x(mx), 0, 0, sub == 0)
    myn, mys = blank(next_y(my), 1, 3, lane16 == 15), blank(last_y(my), 1, 0, lane16 == 0)
    ce, cw, cn, cs = four * (mx + mxe), four * (mx + mxw), four * (my + myn), four * (my + mys)
    cu, cl = four * (mz + next_z(mz)), four * (mz + last_z(mz))
    c4[6] = ce + cw + cn + cs + cu + cl
    c4[0] = blank(ce, 0, 3, sub == 7)
    c4[1] = blank(cw, 0, 0, sub == 0)
    c4[2] = blank(cn, 1, 3, lane16 == 15)
    c4[3] = blank(cs, 1, 0, lane16 == 0)
    c4[4] = cu
    c4[5] = cl

    pieces(lines, 15, recv.at[4])
    fb[xc, yc] = jnp.where((lane & 8) == 0, fa[0], fa[1])
    for target in plane:
        send(fb.at[xc, yc], fb.at[xc, yc], recv.at[5], target, 15)

    rv3[7] = jnp.where(part == 0, vb3[4, 0], jnp.where(part == 1, vb3[5, 0], jnp.where(part == 2, f3[4, 0], f3[5, 0])))
    for dx, dy in wide:
        send(rv3.at[7], rv3.at[7 - dx * 3 - dy], recv.at[6], beside(dx, dy), 16)
    for row in range(8):
        rv1[1, 4 + row] = jnp.where((lane & 1) == 0, vb1[4 + row, 0], f1[4 + row, 0])
    for dx in (-1, 0, 1):
        for dy in (-1, 0, 1):
            if (dx, dy) != (0, 0):
                a, b, c = ((4, 4, 12), (4, 8, 4), (8, 4, 0))[dx + 1]
                send(rv1.at[1, pl.ds(a, b)], rv1.at[1 - dy, pl.ds(c, b)], recv.at[7], beside(dx, dy), 17)

    pieces(tiles, 15, recv.at[5])

    def total(x):
        tile = jnp.sum(x, axis=(0, 1))
        return jnp.sum(jnp.sum(tile, axis=0, keepdims=True), axis=1, keepdims=True)

    def image_of(p):
        out = c4[6] * p - c4[0] * next_x(p) - c4[1] * last_x(p)
        out = out - c4[2] * next_y(p) - c4[3] * last_y(p)
        return out - c4[4] * next_z(p) - c4[5] * last_z(p)

    r = fb[...]
    p = q = v = rr = alpha = None
    for sweep in range(SWEEPS):
        image = image_of(r)
        new, power = total(r * r), total(r * image)
        if sweep == 0:
            p, q, alpha = r, image, new / power
            v = alpha * p
        else:
            beta = new / rr
            alpha = new / (power - beta * new / alpha)
            p = r + beta * p
            q = image + beta * q
            v = v + alpha * p
        rr = new
        if sweep + 1 < SWEEPS:
            r = r - alpha * q
    v4[...] = v

    main_index = sub * 16 + cc * 8 + (lane >> 4)
    side_index = sub * 16 + ((cc * 8 + 8 + (lane >> 4)) & 15)
    other_y = jnp.clip(yc + 2 * cc - 1, 0, 3)
    near = jnp.logical_xor(lane < 64, cc == 1)
    pieces(tiles, 14, recv.at[6])
    octs = [(lane & ~7) + j for j in range(4)]
    for d in range(-2, 3):
        x = jnp.clip(gx + d, 0, NGX - 1)
        here = jnp.broadcast_to(v4[x >> 3, yc, pl.ds(x & 7, 1)], (8, 128))
        there = jnp.broadcast_to(v4[x >> 3, other_y, pl.ds(x & 7, 1)], (8, 128))
        main = pick(here, main_index)
        side = jnp.where(near, pick(here, side_index), pick(there, side_index)) * mask2
        block = (d + 2) * 3
        packed = (rv3[block + 1], jnp.where(lane < 64, rv3[block + 2], rv3[block]))
        inside = row_inside(3, 2 * d)
        for j in range(2):
            row = 2 * d + j
            for p_no in range(2):
                value = pick(packed[p_no], octs[j])
                if p_no == 1:
                    value = value * mask2
                value = value + (main if p_no == 0 else side)
                va3[row + 4, p_no] = value if inside is None else value * inside
                if -3 <= row < 5:
                    f3[row + 4, p_no] = pick(packed[p_no], octs[2 + j])
    field(3, va3, into(vb3, 3), -3, 5, rows_of(f3, 3), True)
    field(3, vb3, into(va3, 3), -2, 4, rows_of(f3, 3), True)

    def refined(ref, level, a, b):
        x = ref[a + LOW[level]:b + LOW[level]]
        return jnp.stack([x, x], axis=1).reshape((2 * (b - a),) + x.shape[1:])

    def correct(level, a, b):
        low = LOW[level]
        for n in range(a, b, 4):
            m = min(n + 4, b)
            VA[level][n + low:m + low] = VB[level][n + low:m + low] + refined(VA[level + 1], level + 1, n // 2, m // 2)

    correct(2, -4, 8)
    field(2, va2, into(vb2, 2), -3, 7, rows_of(f2, 2), True)
    field(2, vb2, into(va2, 2), -2, 6, rows_of(f2, 2), True)

    pieces(tiles, 40, recv.at[7])
    evens, odds = lane & ~1, lane | 1
    for row in range(-4, 12):
        inside = row_inside(1, row)
        if inside is not None:
            value = pick(rv1[1, row + 4], evens)
            vb1[row + 4, 0] = value * inside
            f1[row + 4, 0] = pick(rv1[1, row + 4], odds)
        packed = jnp.where(lane < 64, rv1[2, row + 4], rv1[0, row + 4])
        value = pick(packed, evens) * mask0
        vb1[row + 4, 1] = value if inside is None else value * inside
        f1[row + 4, 1] = pick(packed, odds)
    correct(1, -4, 12)
    field(1, va1, into(vb1, 1), -3, 11, rows_of(f1, 1), True)
    field(1, vb1, into(va1, 1), -2, 10, rows_of(f1, 1), True)

    for a in range(-2, 9):
        lo = -3 if a == -2 else 2 * a
        hi = 2 * a + 2
        add = va1[a + 4]
        for row in range(lo, hi):
            va0[row + 8] = vb0[row + 8] + add
    va0[18 + 8] = vb0[18 + 8] + va1[9 + 4]
    field(0, va0, into(vb0, 0), -2, 18, arr0(1), True)

    def out_stream(a, b, value):
        va0[a + 8:b + 8] = value
        for row in range(max(a, 0), min(b, 16)):
            s_ref[pl.ds(row, 8, 16), :] = value[row - a, 0]

    def out_residual(a, b, value):
        for row in range(a, b):
            q_ref[pl.ds(row, 8, 16), :] = value[row - a, 0]

    field(0, vb0, out_stream, -1, 17, arr0(1), True)
    field(0, va0, out_residual, 0, 16, arr0(1), False)

    for copy in sends:
        copy.wait_send()
    for group, (kind, count) in enumerate(
            ((tiles, 42), (lines, 45), (tiles, 14), (tiles, 45), (lines, 15), (tiles, 15), (tiles, 14), (tiles, 40))):
        pieces(kind, count, ssem.at[10 + group])


def level_scratch():
    shapes = []
    for level in range(4):
        shapes.append(pltpu.VMEM((ROWS[level], 2, 8, 128), F32))
    return shapes


def on_device(vorticity, metric):
    depth, rows, columns = vorticity.shape
    tile = (8, 128)
    scratch = [
        pltpu.VMEM((4, 32, 2) + tile, F32), pltpu.VMEM((3, 16, 2) + tile, F32),
        pltpu.VMEM((4, 128, 128), jnp.bfloat16),
        pltpu.VMEM((depth * rows, columns), F32), pltpu.VMEM((3 * depth * rows, columns), F32),
        pltpu.SemaphoreType.DMA((2,)),
        pltpu.VMEM((4,) + tile, F32), pltpu.VMEM((4,) + tile, F32),
        pltpu.VMEM((8,) + tile, F32), pltpu.VMEM((8,) + tile, F32),
        pltpu.VMEM((15, 3) + tile, F32), pltpu.VMEM((15,) + tile, F32),
        pltpu.VMEM((2, 3) + tile, F32), pltpu.VMEM((4, 4, 3) + tile, F32),
        pltpu.VMEM((2,) + tile, F32), pltpu.VMEM((4, 4) + tile, F32),
        pltpu.VMEM((15,) + tile, F32), pltpu.VMEM((3, 16) + tile, F32),
        pltpu.VMEM((4, 4) + tile, F32), pltpu.VMEM((7, 4, 4) + tile, F32),
    ]
    scratch += level_scratch()[1:]
    for _ in range(6):
        scratch += level_scratch()
    scratch += [pltpu.VMEM((45,) + tile, F32), pltpu.VMEM((45, 1, 128), F32)]
    scratch += [pltpu.SemaphoreType.DMA((18,)), pltpu.SemaphoreType.DMA((10,)), pltpu.SemaphoreType.DMA((8,))]
    flat = jax.ShapeDtypeStruct((depth * rows, columns), F32)
    vmem = pl.BlockSpec(memory_space=pltpu.VMEM)
    stream, residual = pl.pallas_call(
        kernel,
        out_shape=(flat, flat),
        in_specs=[pl.BlockSpec(memory_space=pl.ANY)] * 2,
        out_specs=(vmem, vmem),
        scratch_shapes=scratch,
        compiler_params=pltpu.CompilerParams(collective_id=0, has_side_effects=True, vmem_limit_bytes=48 * 1024 * 1024),
    )(vorticity.reshape(depth * rows, columns), metric.reshape(3 * depth * rows, columns))
    return stream.reshape(vorticity.shape), residual.reshape(vorticity.shape)


def solution(mesh):
    return jax.shard_map(
        on_device,
        mesh=mesh,
        in_specs=(P(None, "gx", "gy"), P(None, None, "gx", "gy")),
        out_specs=(P(None, "gx", "gy"), P(None, "gx", "gy")),
        check_vma=False,
    )
```

```python
import jax
import jax.numpy as jnp
from jax import lax
from jax.experimental import pallas as pl
from jax.experimental.pallas import tpu as pltpu
from jax.sharding import PartitionSpec as P

MESH = pl.DeviceIdType.MESH
NGX, NGY = 32, 8
OMEGA = 0.8
SPAN = 0.25**4
SWEEPS = 8
F32 = jnp.float32

LOW = (8, 4, 8, 4)
ROWS = (32, 16, 20, 10)


def lanes():
    return lax.broadcasted_iota(jnp.int32, (8, 128), 1)


def swap(x):
    return jnp.concatenate([x[:, 1:2], x[:, 0:1]], axis=1)


def north(x, step):
    turned = pltpu.roll(x, 128 - step, 3)
    return jnp.where(lanes() >= 128 - step, swap(turned), turned)


def south(x, step):
    turned = pltpu.roll(x, step, 3)
    return jnp.where(lanes() < step, swap(turned), turned)


def upper(x):
    return pltpu.roll(x, 7, x.ndim - 2)


def lower(x):
    return pltpu.roll(x, 1, x.ndim - 2)


def operate(v, cx, cy, cz, step):
    fx = cx * (v[:-1] - v[1:])
    mid = v[1:-1]
    fy = cy * (mid - north(mid, step))
    fz = cz * (mid - upper(mid))
    return (fx[1:] - fx[:-1]) + (fy - south(fy, step)) + (fz - lower(fz))


def coarsen_field(x, step):
    y = x.reshape((x.shape[0] // 2, 2) + x.shape[1:])
    both, axis = y[:, 0] + y[:, 1], x.ndim - 1
    other = jnp.where((lanes() & step) == 0, pltpu.roll(both, 128 - step, axis), pltpu.roll(both, step, axis))
    return 0.25 * (both + other)


def moved(x, matrix):
    first = x.astype(jnp.bfloat16)
    rest = x - first.astype(F32)
    second = rest.astype(jnp.bfloat16)
    third = (rest - second.astype(F32)).astype(jnp.bfloat16)
    terms = [jnp.dot(term, matrix, preferred_element_type=F32) for term in (first, second, third)]
    return terms[0] + (terms[1] + terms[2])


def pick(x, index):
    return jnp.take_along_axis(x, index, axis=1)


def kernel(f_ref, m_ref, s_ref, q_ref,
           e0, m1, pairs, f_in, m_in, in_sem, kr, kl, rkl, rkr, rm2, rf2, ma, mb, fa, fb, rv3, rv1, v4, c4,
           f1, f2, f3, w0, w1, w2, w3, cx0, cx1, cx2, cx3, cy0, cy1, cy2, cy3, cz0, cz1, cz2, cz3,
           va0, va1, va2, va3, vb0, vb1, vb2, vb3,
           tiles, lines, ssem, r1_sem, recv):
    gx, gy = lax.axis_index("gx"), lax.axis_index("gy")
    xc, zc = gx >> 3, gx & 7
    yc, cc = gy >> 1, gy & 1
    CX, CY, CZ, W = (cx0, cx1, cx2, cx3), (cy0, cy1, cy2, cy3), (cz0, cz1, cz2, cz3), (w0, w1, w2, w3)
    VA, VB = (va0, va1, va2, va3), (vb0, vb1, vb2, vb3)
    lane = lanes()
    sub = lax.broadcasted_iota(jnp.int32, (8, 128), 0)
    slot = lane >> 3

    def beside(dx, dy):
        return ((gx + dx + NGX) % NGX, (gy + dy + NGY) % NGY)

    wide = [(dx, dy) for dx in (-2, -1, 0, 1, 2) for dy in (-1, 0, 1) if (dx, dy) != (0, 0)]
    column = [(xc * 8 + (zc + dz) % 8, yc * 2 + (cc + dc) % 2) for dz in range(8) for dc in range(2) if (dz, dc) != (0, 0)]
    plane = [(((xc + dx) % 4) * 8 + zc, ((yc + dy) % 4) * 2 + cc) for dx in range(4) for dy in range(4) if (dx, dy) != (0, 0)]

    def pair_mean(total, step):
        return moved(total.reshape(-1, 128), pairs[step.bit_length() - 1]).reshape(total.shape)

    def coarsen(x, step):
        y = x.reshape((x.shape[0] // 2, 2) + x.shape[1:])
        return pair_mean(y[:, 0] + y[:, 1], step)

    barrier = pltpu.get_barrier_semaphore()
    everyone = [beside(dx, dy) for dx, dy in wide] + column + plane
    for target in everyone:
        pl.semaphore_signal(barrier, inc=1, device_id=target, device_id_type=MESH)

    def send(src, dst, sem, to, out):
        copy = pltpu.make_async_remote_copy(
            src_ref=src, dst_ref=dst, send_sem=ssem.at[out], recv_sem=sem, device_id=to, device_id_type=MESH)
        copy.start()
        return copy

    def pieces(kind, count, sem):
        ref = kind.at[pl.ds(0, count)]
        pltpu.make_async_copy(ref, ref, sem).wait()

    source = lax.broadcasted_iota(jnp.int32, (128, 128), 0)
    goal = lax.broadcasted_iota(jnp.int32, (128, 128), 1)

    def matrix_of(condition, value=1.0):
        return jnp.where(condition, value, 0.0).astype(jnp.bfloat16)

    loads = [pltpu.make_async_copy(m_ref, m_in, in_sem.at[0]), pltpu.make_async_copy(f_ref, f_in, in_sem.at[1])]
    for copy in loads:
        copy.start()
    for copy in loads:
        copy.wait()

    for row in range(16):
        for arr in range(4):
            if arr == 1:
                tile = f_in[pl.ds(row, 8, 16), :]
            else:
                tile = m_in[pl.ds((arr - 1 if arr else 0) * 128 + row, 8, 16), :]
            e0[arr, 8 + row, 0] = tile
    for k in range(4):
        right, left = jnp.zeros((8, 128), F32), jnp.zeros((8, 128), F32)
        for g in range(16):
            turned = pltpu.roll(e0[g % 4, 8 + 4 * k + g // 4, 0], (8 * g + 8) % 128, 1)
            right = jnp.where(slot == g, turned, right)
            left = jnp.where(slot == (g + 1) % 16, turned, left)
        kr[k] = right
        kl[k] = left

    turn = yc + 4 * (xc >> 1)

    def spread_row(tile):
        turned = pick(tile, 16 * (lane & 7))
        return jnp.sum(jnp.where(sub == (((lane >> 4) - turn) & 7), turned, 0.0), axis=0, keepdims=True)

    pl.semaphore_wait(barrier, len(everyone))

    sends = []
    east, west = beside(1, 0), beside(-1, 0)
    rest = pl.ds(1, 3)
    sends.append(send(e0.at[0, pl.ds(16, 8), 0], e0.at[0, pl.ds(0, 8), 0], r1_sem.at[0], east, 0))
    sends.append(send(e0.at[0, pl.ds(8, 8), 0], e0.at[0, pl.ds(24, 8), 0], r1_sem.at[1], west, 1))
    sends.append(send(e0.at[rest, pl.ds(18, 6), 0], e0.at[rest, pl.ds(2, 6), 0], r1_sem.at[2], east, 2))
    sends.append(send(e0.at[rest, pl.ds(8, 6), 0], e0.at[rest, pl.ds(24, 6), 0], r1_sem.at[3], west, 3))
    for side, (packed, into) in enumerate(((kr, rkl), (kl, rkr))):
        dy = 1 - 2 * side
        for n, (dx, a, b, c) in enumerate(((1, 2, 2, 0), (-1, 0, 2, 6), (0, 0, 4, 2))):
            at = 4 + 3 * side + n
            sends.append(send(packed.at[pl.ds(a, b)], into.at[pl.ds(c, b)], r1_sem.at[at], beside(dx, dy), at))
    for n in range(4):
        pairs[n] = matrix_of(jnp.logical_or(source == goal, source == (goal ^ (1 << n))), 0.25)
    for comp in range(3):
        arr = (0, 2, 3)[comp]
        m2 = coarsen(coarsen(e0[arr, 8:24, 0], 1), 2)
        m3 = coarsen(m2, 4)
        m4 = coarsen(m3, 8)
        part = lane & 3
        rm2[7, comp] = jnp.where(part == 0, m2[0], jnp.where(part == 1, m2[1], jnp.where(part == 2, m2[2], m2[3])))
        ma[cc, comp, pl.ds(zc, 1)] = spread_row(m4[0])

    for dx, dy in wide:
        send(rm2.at[7], rm2.at[7 - dx * 3 - dy], recv.at[0], beside(dx, dy), 10)
    for target in column:
        mine = ma.at[cc, pl.ds(0, 3), pl.ds(zc, 1)]
        send(mine, mine, recv.at[1], target, 11)
    for copy in sends:
        copy.wait_recv()

    even = (lane & 8) == 0
    for k in range(8):
        me = jnp.where(even, rkl[k], rkr[k])
        mo = jnp.where(even, rkr[k], rkl[k])
        for g in range(16):
            e0[g % 4, 4 * k + g // 4, 1] = pltpu.roll(me if g % 2 == 0 else mo, (120 - 8 * g) % 128, 1)

    has_left, has_right = gy > 0, gy < NGY - 1

    def side_mask(reach):
        inside = jnp.logical_or(jnp.logical_and(lane < reach, has_right), jnp.logical_and(lane >= 128 - reach, has_left))
        return inside.astype(F32)

    mask0, mask2 = side_mask(8), side_mask(64)

    def row_inside(level, row):
        own = 16 >> level
        if row < 0:
            need = -(row // own)
            return (gx >= need).astype(F32)
        if row >= own:
            return (gx + row // own <= NGX - 1).astype(F32)
        return None

    def masked(tile, level, row, part):
        side = mask0 if level < 2 else mask2
        scale = row_inside(level, row)
        if part == 1:
            tile = tile * side
        return tile if scale is None else tile * scale

    for arr in (0, 2, 3):
        for row in range(-8 if arr == 0 else -6, 24 if arr == 0 else 22):
            for part in range(2):
                if part == 1 or row < 0 or row >= 16:
                    e0[arr, row + 8, part] = masked(e0[arr, row + 8, part], 0, row, part)

    def coefficients(level, mx, my, mz, lo, hi):
        low, step = LOW[level], 1 << level
        half, spans = 0.5 * 0.25**level, 0.5 * SPAN
        for a in range(lo, hi, 4):
            b = min(a + 4, hi)
            x = mx(a - 1, b + 1)
            cx = half * (x[:-1] + x[1:])
            y = my(a, b)
            cy = half * (y + north(y, step))
            z = mz(a, b)
            cz = spans * (z + upper(z))
            CX[level][a - 1 + low:b + low] = cx
            CY[level][a + low:b + low] = cy
            CZ[level][a + low:b + low] = cz
            diag = cx[:-1] + cx[1:] + cy + south(cy, step) + cz + lower(cz)
            w = OMEGA / diag
            for row in range(a, b):
                for part in range(2):
                    tile = w[row - a, part]
                    side = mask0 if level < 2 else mask2
                    scale = row_inside(level, row)
                    if part == 1:
                        tile = jnp.where(side > 0, tile, 0.0)
                    if scale is not None:
                        tile = jnp.where(scale > 0, tile, 0.0)
                    W[level][row + low, part] = tile

    def field(level, source, target, lo, hi, f_of, relax, chunk=4):
        low, step = LOW[level], 1 << level
        for a in range(lo, hi, chunk):
            b = min(a + chunk, hi)
            v = source[a - 1 + low:b + 1 + low]
            left = f_of(a, b) - operate(
                v, CX[level][a - 1 + low:b + low], CY[level][a + low:b + low], CZ[level][a + low:b + low], step)
            target(a, b, v[1:-1] + W[level][a + low:b + low] * left if relax else left)

    def into(ref, level):
        def store(a, b, value):
            ref[a + LOW[level]:b + LOW[level]] = value
        return store

    def into_coarse(ref, level):
        def store(a, b, value):
            ref[a // 2 + LOW[level + 1]:b // 2 + LOW[level + 1]] = coarsen_field(value, 1 << level)
        return store

    def rows_of(ref, level):
        return lambda a, b: ref[a + LOW[level]:b + LOW[level]]

    def start(level, f_of, lo, hi):
        low = LOW[level]
        for a in range(lo, hi, 4):
            b = min(a + 4, hi)
            VA[level][a + low:b + low] = W[level][a + low:b + low] * f_of(a, b)

    def arr0(arr):
        return lambda a, b: e0[arr, a + 8:b + 8]

    coefficients(0, arr0(0), arr0(2), arr0(3), -6, 22)
    start(0, arr0(1), -6, 22)
    field(0, va0, into(vb0, 0), -5, 21, arr0(1), True)
    field(0, vb0, into_coarse(f1, 0), -4, 20, arr0(1), False)

    for comp, arr in enumerate((0, 2, 3)):
        lo, hi = (-4, 12) if arr == 0 else (-3, 11)
        m1[comp, lo + 4:hi + 4] = coarsen(e0[arr, 2 * lo + 8:2 * hi + 8], 1)

    def coarse1(comp):
        return lambda a, b: m1[comp, a + 4:b + 4]

    coefficients(1, coarse1(0), coarse1(1), coarse1(2), -3, 11)
    start(1, rows_of(f1, 1), -2, 10)
    field(1, va1, into(vb1, 1), -1, 9, rows_of(f1, 1), True)
    own2 = []

    def keep(a, b, value):
        own2.append(coarsen_field(value[:, 0], 2))

    field(1, vb1, keep, 0, 8, rows_of(f1, 1), False)
    part = lane & 3
    rf2[7] = jnp.where(part == 0, own2[0][0], jnp.where(part == 1, own2[0][1], jnp.where(part == 2, own2[1][0], own2[1][1])))
    for dx, dy in wide:
        send(rf2.at[7], rf2.at[7 - dx * 3 - dy], recv.at[2], beside(dx, dy), 12)

    pieces(tiles, 42, recv.at[0])
    quads = [(lane & ~3) + j for j in range(4)]

    def rows2(of, a, b):
        out = []
        for row in range(a, b):
            block = (row // 4 + 2) * 3
            main = of(block + 1)
            side = jnp.where(lane < 64, of(block + 2), of(block))
            out.append(jnp.stack([pick(main, quads[row % 4]), pick(side, quads[row % 4])]))
        return jnp.stack(out)

    def metric2(comp):
        def rows(a, b):
            got = rows2(lambda slot: rm2[slot, comp], a, b)
            return jnp.stack([jnp.stack([masked(got[n, p], 2, a + n, p) for p in range(2)]) for n in range(b - a)])
        return rows

    def metric3(comp):
        return lambda a, b: coarsen(metric2(comp)(2 * a, 2 * b), 4)

    coefficients(2, metric2(0), metric2(1), metric2(2), -7, 11)
    coefficients(3, metric3(0), metric3(1), metric3(2), -3, 5)

    pieces(tiles, 14, recv.at[2])
    pieces(lines, 45, recv.at[1])
    own4 = [jnp.where((lane & 8) == 0, ma[0, comp], ma[1, comp]) for comp in range(3)]
    for comp in range(3):
        mb[xc, yc, comp] = own4[comp]
    for target in plane:
        send(mb.at[xc, yc], mb.at[xc, yc], recv.at[3], target, 13)

    for a in range(-6, 10, 4):
        f2[a + 8:a + 12] = rows2(lambda slot: rf2[slot], a, a + 4)
    start(2, rows_of(f2, 2), -6, 10)
    field(2, va2, into(vb2, 2), -5, 9, rows_of(f2, 2), True)
    field(2, vb2, into_coarse(f3, 2), -4, 8, rows_of(f2, 2), False)
    start(3, rows_of(f3, 3), -2, 4)
    field(3, va3, into(vb3, 3), -1, 3, rows_of(f3, 3), True)
    own4f = []

    def keep4(a, b, value):
        own4f.append(coarsen_field(value[:, 0], 8))

    field(3, vb3, keep4, 0, 2, rows_of(f3, 3), False)
    fa[cc, pl.ds(zc, 1)] = spread_row(own4f[0][0])
    for target in column:
        mine = fa.at[cc, pl.ds(zc, 1)]
        send(mine, mine, recv.at[4], target, 14)

    pieces(lines, 15, recv.at[4])
    fb[xc, yc] = jnp.where((lane & 8) == 0, fa[0], fa[1])
    for target in plane:
        send(fb.at[xc, yc], fb.at[xc, yc], recv.at[5], target, 15)

    rv3[7] = jnp.where(part == 0, vb3[4, 0], jnp.where(part == 1, vb3[5, 0], jnp.where(part == 2, f3[4, 0], f3[5, 0])))
    for dx, dy in wide:
        send(rv3.at[7], rv3.at[7 - dx * 3 - dy], recv.at[6], beside(dx, dy), 16)
    for row in range(8):
        rv1[1, 4 + row] = jnp.where((lane & 1) == 0, vb1[4 + row, 0], f1[4 + row, 0])
    for dx in (-1, 0, 1):
        for dy in (-1, 0, 1):
            if (dx, dy) != (0, 0):
                a, b, c = ((4, 4, 12), (4, 8, 4), (8, 4, 0))[dx + 1]
                send(rv1.at[1, pl.ds(a, b)], rv1.at[1 - dy, pl.ds(c, b)], recv.at[7], beside(dx, dy), 17)

    pieces(tiles, 45, recv.at[3])
    four = 0.5 * 0.25**4
    column_y = lane & 63
    first_half = lane < 64
    whose = ((lane >> 4) - sub) & 7
    unturn = (lane + 16 * sub) & 127

    def whole(row_of):
        out = []
        for r in range(16):
            mixed = None
            for k in range(8):
                row = jnp.broadcast_to(row_of((r >> 3) + 2 * (k >> 2), k & 3, r & 7), (8, 128))
                mixed = row if k == 0 else jnp.where(whose == k, row, mixed)
            out.append(pick(mixed, unturn))
        return jnp.stack(out)

    def next_x(v):
        return jnp.concatenate([v[1:], jnp.where(first_half, pltpu.roll(v[0:1], 64, 2), 0.0)], axis=0)

    def last_x(v):
        return jnp.concatenate([jnp.where(first_half, 0.0, pltpu.roll(v[15:16], 64, 2)), v[:-1]], axis=0)

    def next_y(v):
        return pltpu.roll(v, 127, 2)

    def last_y(v):
        return pltpu.roll(v, 1, 2)

    mx, my, mz = [whole(lambda a, b, c, comp=comp: mb[a, b, comp, c:c + 1]) for comp in range(3)]
    ce, cw = four * (mx + next_x(mx)), four * (mx + last_x(mx))
    cn = four * (my + jnp.where(column_y == 63, 0.0, next_y(my)))
    cs = four * (my + jnp.where(column_y == 0, 0.0, last_y(my)))
    cu, cl = four * (mz + upper(mz)), four * (mz + lower(mz))
    c4[0] = ce
    c4[1] = cw
    c4[2] = jnp.where(column_y == 63, 0.0, cn)
    c4[3] = jnp.where(column_y == 0, 0.0, cs)
    c4[4] = cu
    c4[5] = cl
    c4[6] = ce + cw + cn + cs + cu + cl

    pieces(tiles, 15, recv.at[5])

    def total(x):
        tile = jnp.sum(x, axis=0)
        return jnp.sum(jnp.sum(tile, axis=0, keepdims=True), axis=1, keepdims=True)

    def image_of(p):
        out = c4[6] * p - c4[0] * next_x(p) - c4[1] * last_x(p)
        out = out - c4[2] * next_y(p) - c4[3] * last_y(p)
        return out - c4[4] * upper(p) - c4[5] * lower(p)

    r = whole(lambda a, b, c: fb[a, b, c:c + 1])
    p = q = v = rr = alpha = None
    for sweep in range(SWEEPS):
        image = image_of(r)
        new, power = total(r * r), total(r * image)
        if sweep == 0:
            p, q, alpha = r, image, new / power
            v = alpha * p
        else:
            beta = new / rr
            alpha = new / (power - beta * new / alpha)
            p = r + beta * p
            q = image + beta * q
            v = v + alpha * p
        rr = new
        if sweep + 1 < SWEEPS:
            r = r - alpha * q
    v4[...] = v

    pieces(tiles, 14, recv.at[6])
    octs = [(lane & ~7) + j for j in range(4)]
    for d in range(-2, 3):
        x = jnp.clip(gx + d, 0, NGX - 1)
        tile = v4[x & 15]
        half = (x >> 4) * 64
        main = pick(tile, half + gy * 8 + (lane >> 4))
        side = pick(tile, half + ((gy * 8 + jnp.where(first_half, 8, -8) + (lane >> 4)) & 63)) * mask2
        block = (d + 2) * 3
        packed = (rv3[block + 1], jnp.where(lane < 64, rv3[block + 2], rv3[block]))
        inside = row_inside(3, 2 * d)
        for j in range(2):
            row = 2 * d + j
            for p_no in range(2):
                value = pick(packed[p_no], octs[j])
                if p_no == 1:
                    value = value * mask2
                value = value + (main if p_no == 0 else side)
                va3[row + 4, p_no] = value if inside is None else value * inside
                if -3 <= row < 5:
                    f3[row + 4, p_no] = pick(packed[p_no], octs[2 + j])
    field(3, va3, into(vb3, 3), -3, 5, rows_of(f3, 3), True)
    field(3, vb3, into(va3, 3), -2, 4, rows_of(f3, 3), True)

    def refined(ref, level, a, b):
        x = ref[a + LOW[level]:b + LOW[level]]
        return jnp.stack([x, x], axis=1).reshape((2 * (b - a),) + x.shape[1:])

    def correct(level, a, b):
        low = LOW[level]
        for n in range(a, b, 4):
            m = min(n + 4, b)
            VA[level][n + low:m + low] = VB[level][n + low:m + low] + refined(VA[level + 1], level + 1, n // 2, m // 2)

    correct(2, -4, 8)
    field(2, va2, into(vb2, 2), -3, 7, rows_of(f2, 2), True)
    field(2, vb2, into(va2, 2), -2, 6, rows_of(f2, 2), True)

    pieces(tiles, 40, recv.at[7])
    evens, odds = lane & ~1, lane | 1
    for row in range(-4, 12):
        inside = row_inside(1, row)
        if inside is not None:
            value = pick(rv1[1, row + 4], evens)
            vb1[row + 4, 0] = value * inside
            f1[row + 4, 0] = pick(rv1[1, row + 4], odds)
        packed = jnp.where(lane < 64, rv1[2, row + 4], rv1[0, row + 4])
        value = pick(packed, evens) * mask0
        vb1[row + 4, 1] = value if inside is None else value * inside
        f1[row + 4, 1] = pick(packed, odds)
    correct(1, -4, 12)
    field(1, va1, into(vb1, 1), -3, 11, rows_of(f1, 1), True)
    field(1, vb1, into(va1, 1), -2, 10, rows_of(f1, 1), True)

    for a in range(-2, 9):
        lo = -3 if a == -2 else 2 * a
        hi = 2 * a + 2
        add = va1[a + 4]
        for row in range(lo, hi):
            va0[row + 8] = vb0[row + 8] + add
    va0[18 + 8] = vb0[18 + 8] + va1[9 + 4]
    field(0, va0, into(vb0, 0), -2, 18, arr0(1), True)

    def out_stream(a, b, value):
        va0[a + 8:b + 8] = value
        for row in range(max(a, 0), min(b, 16)):
            s_ref[pl.ds(row, 8, 16), :] = value[row - a, 0]

    def out_residual(a, b, value):
        for row in range(a, b):
            q_ref[pl.ds(row, 8, 16), :] = value[row - a, 0]

    field(0, vb0, out_stream, -1, 17, arr0(1), True)
    field(0, va0, out_residual, 0, 16, arr0(1), False)

    for copy in sends:
        copy.wait_send()
    for group, (kind, count) in enumerate(
            ((tiles, 42), (lines, 45), (tiles, 14), (tiles, 45), (lines, 15), (tiles, 15), (tiles, 14), (tiles, 40))):
        pieces(kind, count, ssem.at[10 + group])


def level_scratch():
    shapes = []
    for level in range(4):
        shapes.append(pltpu.VMEM((ROWS[level], 2, 8, 128), F32))
    return shapes


def on_device(vorticity, metric):
    depth, rows, columns = vorticity.shape
    tile = (8, 128)
    scratch = [
        pltpu.VMEM((4, 32, 2) + tile, F32), pltpu.VMEM((3, 16, 2) + tile, F32),
        pltpu.VMEM((4, 128, 128), jnp.bfloat16),
        pltpu.VMEM((depth * rows, columns), F32), pltpu.VMEM((3 * depth * rows, columns), F32),
        pltpu.SemaphoreType.DMA((2,)),
        pltpu.VMEM((4,) + tile, F32), pltpu.VMEM((4,) + tile, F32),
        pltpu.VMEM((8,) + tile, F32), pltpu.VMEM((8,) + tile, F32),
        pltpu.VMEM((15, 3) + tile, F32), pltpu.VMEM((15,) + tile, F32),
        pltpu.VMEM((2, 3) + tile, F32), pltpu.VMEM((4, 4, 3) + tile, F32),
        pltpu.VMEM((2,) + tile, F32), pltpu.VMEM((4, 4) + tile, F32),
        pltpu.VMEM((15,) + tile, F32), pltpu.VMEM((3, 16) + tile, F32),
        pltpu.VMEM((16,) + tile, F32), pltpu.VMEM((7, 16) + tile, F32),
    ]
    scratch += level_scratch()[1:]
    for _ in range(6):
        scratch += level_scratch()
    scratch += [pltpu.VMEM((45,) + tile, F32), pltpu.VMEM((45, 1, 128), F32)]
    scratch += [pltpu.SemaphoreType.DMA((18,)), pltpu.SemaphoreType.DMA((10,)), pltpu.SemaphoreType.DMA((8,))]
    flat = jax.ShapeDtypeStruct((depth * rows, columns), F32)
    vmem = pl.BlockSpec(memory_space=pltpu.VMEM)
    stream, residual = pl.pallas_call(
        kernel,
        out_shape=(flat, flat),
        in_specs=[pl.BlockSpec(memory_space=pl.ANY)] * 2,
        out_specs=(vmem, vmem),
        scratch_shapes=scratch,
        compiler_params=pltpu.CompilerParams(collective_id=0, has_side_effects=True, vmem_limit_bytes=48 * 1024 * 1024),
    )(vorticity.reshape(depth * rows, columns), metric.reshape(3 * depth * rows, columns))
    return stream.reshape(vorticity.shape), residual.reshape(vorticity.shape)


def solution(mesh):
    return jax.shard_map(
        on_device,
        mesh=mesh,
        in_specs=(P(None, "gx", "gy"), P(None, None, "gx", "gy")),
        out_specs=(P(None, "gx", "gy"), P(None, "gx", "gy")),
        check_vma=False,
    )
```

```python
import jax
import jax.numpy as jnp
from jax import lax
from jax.experimental import pallas as pl
from jax.experimental.pallas import tpu as pltpu
from jax.sharding import PartitionSpec as P

MESH = pl.DeviceIdType.MESH
NGX, NGY = 32, 8
OMEGA = 0.8
SPAN = 0.25**4
SWEEPS = 8
F32 = jnp.float32

LOW = (8, 4, 8, 4)
ROWS = (32, 16, 20, 10)


def lanes():
    return lax.broadcasted_iota(jnp.int32, (8, 128), 1)


def swap(x):
    return jnp.concatenate([x[:, 1:2], x[:, 0:1]], axis=1)


def north(x, step):
    turned = pltpu.roll(x, 128 - step, 3)
    return jnp.where(lanes() >= 128 - step, swap(turned), turned)


def south(x, step):
    turned = pltpu.roll(x, step, 3)
    return jnp.where(lanes() < step, swap(turned), turned)


def upper(x):
    return pltpu.roll(x, 7, x.ndim - 2)


def lower(x):
    return pltpu.roll(x, 1, x.ndim - 2)


def operate(v, cx, cy, cz, step):
    fx = cx * (v[:-1] - v[1:])
    mid = v[1:-1]
    fy = cy * (mid - north(mid, step))
    fz = cz * (mid - upper(mid))
    return (fx[1:] - fx[:-1]) + (fy - south(fy, step)) + (fz - lower(fz))


def coarsen_field(x, step):
    y = x.reshape((x.shape[0] // 2, 2) + x.shape[1:])
    both, axis = y[:, 0] + y[:, 1], x.ndim - 1
    other = jnp.where((lanes() & step) == 0, pltpu.roll(both, 128 - step, axis), pltpu.roll(both, step, axis))
    return 0.25 * (both + other)


def moved(x, matrix):
    first = x.astype(jnp.bfloat16)
    rest = x - first.astype(F32)
    second = rest.astype(jnp.bfloat16)
    third = (rest - second.astype(F32)).astype(jnp.bfloat16)
    terms = [jnp.dot(term, matrix, preferred_element_type=F32) for term in (first, second, third)]
    return terms[0] + (terms[1] + terms[2])


def pick(x, index):
    return jnp.take_along_axis(x, index, axis=1)


def kernel(f_ref, m_ref, s_ref, q_ref,
           e0, m1, pairs, f_in, m_in, in_sem, kr, kl, rkl, rkr, rm2, rf2, ma, mb, fa, fb, rv3, rv1, v4, c4,
           f1, f2, f3, w0, w1, w2, w3, cx0, cx1, cx2, cx3, cy0, cy1, cy2, cy3, cz0, cz1, cz2, cz3,
           va0, va1, va2, va3, vb0, vb1, vb2, vb3,
           tiles, lines, ssem, r1_sem, recv):
    gx, gy = lax.axis_index("gx"), lax.axis_index("gy")
    xc, zc = gx >> 3, gx & 7
    yc, cc = gy >> 1, gy & 1
    CX, CY, CZ, W = (cx0, cx1, cx2, cx3), (cy0, cy1, cy2, cy3), (cz0, cz1, cz2, cz3), (w0, w1, w2, w3)
    VA, VB = (va0, va1, va2, va3), (vb0, vb1, vb2, vb3)
    lane = lanes()
    sub = lax.broadcasted_iota(jnp.int32, (8, 128), 0)
    slot = lane >> 3

    def beside(dx, dy):
        return ((gx + dx + NGX) % NGX, (gy + dy + NGY) % NGY)

    wide = [(dx, dy) for dx in (-2, -1, 0, 1, 2) for dy in (-1, 0, 1) if (dx, dy) != (0, 0)]
    column = [(xc * 8 + (zc + dz) % 8, yc * 2 + (cc + dc) % 2) for dz in range(8) for dc in range(2) if (dz, dc) != (0, 0)]
    plane = [(((xc + dx) % 4) * 8 + zc, ((yc + dy) % 4) * 2 + cc) for dx in range(4) for dy in range(4) if (dx, dy) != (0, 0)]

    def pair_mean(total, step):
        return moved(total.reshape(-1, 128), pairs[step.bit_length() - 1]).reshape(total.shape)

    def coarsen(x, step):
        y = x.reshape((x.shape[0] // 2, 2) + x.shape[1:])
        return pair_mean(y[:, 0] + y[:, 1], step)

    barrier = pltpu.get_barrier_semaphore()
    everyone = [beside(dx, dy) for dx, dy in wide] + column + plane
    for target in everyone:
        pl.semaphore_signal(barrier, inc=1, device_id=target, device_id_type=MESH)

    def send(src, dst, sem, to, out):
        copy = pltpu.make_async_remote_copy(
            src_ref=src, dst_ref=dst, send_sem=ssem.at[out], recv_sem=sem, device_id=to, device_id_type=MESH)
        copy.start()
        return copy

    def pieces(kind, count, sem):
        ref = kind.at[pl.ds(0, count)]
        pltpu.make_async_copy(ref, ref, sem).wait()

    source = lax.broadcasted_iota(jnp.int32, (128, 128), 0)
    goal = lax.broadcasted_iota(jnp.int32, (128, 128), 1)

    def matrix_of(condition, value=1.0):
        return jnp.where(condition, value, 0.0).astype(jnp.bfloat16)

    loads = [pltpu.make_async_copy(m_ref, m_in, in_sem.at[0]), pltpu.make_async_copy(f_ref, f_in, in_sem.at[1])]
    for copy in loads:
        copy.start()
    for copy in loads:
        copy.wait()

    for row in range(16):
        for arr in range(4):
            if arr == 1:
                tile = f_in[pl.ds(row, 8, 16), :]
            else:
                tile = m_in[pl.ds((arr - 1 if arr else 0) * 128 + row, 8, 16), :]
            e0[arr, 8 + row, 0] = tile
    for k in range(4):
        right, left = jnp.zeros((8, 128), F32), jnp.zeros((8, 128), F32)
        for g in range(16):
            turned = pltpu.roll(e0[g % 4, 8 + 4 * k + g // 4, 0], (8 * g + 8) % 128, 1)
            right = jnp.where(slot == g, turned, right)
            left = jnp.where(slot == (g + 1) % 16, turned, left)
        kr[k] = right
        kl[k] = left

    turn = yc + 4 * (xc >> 1)

    def spread_row(tile):
        turned = pick(tile, 16 * (lane & 7))
        return jnp.sum(jnp.where(sub == (((lane >> 4) - turn) & 7), turned, 0.0), axis=0, keepdims=True)

    pl.semaphore_wait(barrier, len(everyone))

    sends = []
    east, west = beside(1, 0), beside(-1, 0)
    rest = pl.ds(1, 3)
    sends.append(send(e0.at[0, pl.ds(16, 8), 0], e0.at[0, pl.ds(0, 8), 0], r1_sem.at[0], east, 0))
    sends.append(send(e0.at[0, pl.ds(8, 8), 0], e0.at[0, pl.ds(24, 8), 0], r1_sem.at[1], west, 1))
    sends.append(send(e0.at[rest, pl.ds(18, 6), 0], e0.at[rest, pl.ds(2, 6), 0], r1_sem.at[2], east, 2))
    sends.append(send(e0.at[rest, pl.ds(8, 6), 0], e0.at[rest, pl.ds(24, 6), 0], r1_sem.at[3], west, 3))
    for side, (packed, into) in enumerate(((kr, rkl), (kl, rkr))):
        dy = 1 - 2 * side
        for n, (dx, a, b, c) in enumerate(((1, 2, 2, 0), (-1, 0, 2, 6), (0, 0, 4, 2))):
            at = 4 + 3 * side + n
            sends.append(send(packed.at[pl.ds(a, b)], into.at[pl.ds(c, b)], r1_sem.at[at], beside(dx, dy), at))
    for n in range(4):
        pairs[n] = matrix_of(jnp.logical_or(source == goal, source == (goal ^ (1 << n))), 0.25)
    for comp in range(3):
        arr = (0, 2, 3)[comp]
        m2 = coarsen(coarsen(e0[arr, 8:24, 0], 1), 2)
        m3 = coarsen(m2, 4)
        m4 = coarsen(m3, 8)
        part = lane & 3
        rm2[7, comp] = jnp.where(part == 0, m2[0], jnp.where(part == 1, m2[1], jnp.where(part == 2, m2[2], m2[3])))
        ma[cc, comp, pl.ds(zc, 1)] = spread_row(m4[0])

    for dx, dy in wide:
        send(rm2.at[7], rm2.at[7 - dx * 3 - dy], recv.at[0], beside(dx, dy), 10)
    for target in column:
        mine = ma.at[cc, pl.ds(0, 3), pl.ds(zc, 1)]
        send(mine, mine, recv.at[1], target, 11)
    for copy in sends:
        copy.wait_recv()

    even = (lane & 8) == 0
    for k in range(8):
        me = jnp.where(even, rkl[k], rkr[k])
        mo = jnp.where(even, rkr[k], rkl[k])
        for g in range(16):
            e0[g % 4, 4 * k + g // 4, 1] = pltpu.roll(me if g % 2 == 0 else mo, (120 - 8 * g) % 128, 1)

    has_left, has_right = gy > 0, gy < NGY - 1

    def side_mask(reach):
        inside = jnp.logical_or(jnp.logical_and(lane < reach, has_right), jnp.logical_and(lane >= 128 - reach, has_left))
        return inside.astype(F32)

    mask0, mask2 = side_mask(8), side_mask(64)

    def row_inside(level, row):
        own = 16 >> level
        if row < 0:
            need = -(row // own)
            return (gx >= need).astype(F32)
        if row >= own:
            return (gx + row // own <= NGX - 1).astype(F32)
        return None

    def masked(tile, level, row, part):
        side = mask0 if level < 2 else mask2
        scale = row_inside(level, row)
        if part == 1:
            tile = tile * side
        return tile if scale is None else tile * scale

    for arr in (0, 2, 3):
        for row in range(-8 if arr == 0 else -6, 24 if arr == 0 else 22):
            for part in range(2):
                if part == 1 or row < 0 or row >= 16:
                    e0[arr, row + 8, part] = masked(e0[arr, row + 8, part], 0, row, part)

    def coefficients(level, mx, my, mz, lo, hi):
        low, step = LOW[level], 1 << level
        half, spans = 0.5 * 0.25**level, 0.5 * SPAN
        for a in range(lo, hi, 4):
            b = min(a + 4, hi)
            x = mx(a - 1, b + 1)
            cx = half * (x[:-1] + x[1:])
            y = my(a, b)
            cy = half * (y + north(y, step))
            z = mz(a, b)
            cz = spans * (z + upper(z))
            CX[level][a - 1 + low:b + low] = cx
            CY[level][a + low:b + low] = cy
            CZ[level][a + low:b + low] = cz
            diag = cx[:-1] + cx[1:] + cy + south(cy, step) + cz + lower(cz)
            w = OMEGA / diag
            for row in range(a, b):
                for part in range(2):
                    tile = w[row - a, part]
                    side = mask0 if level < 2 else mask2
                    scale = row_inside(level, row)
                    if part == 1:
                        tile = jnp.where(side > 0, tile, 0.0)
                    if scale is not None:
                        tile = jnp.where(scale > 0, tile, 0.0)
                    W[level][row + low, part] = tile

    def field(level, source, target, lo, hi, f_of, relax, chunk=4):
        low, step = LOW[level], 1 << level
        for a in range(lo, hi, chunk):
            b = min(a + chunk, hi)
            v = source[a - 1 + low:b + 1 + low]
            left = f_of(a, b) - operate(
                v, CX[level][a - 1 + low:b + low], CY[level][a + low:b + low], CZ[level][a + low:b + low], step)
            target(a, b, v[1:-1] + W[level][a + low:b + low] * left if relax else left)

    def into(ref, level):
        def store(a, b, value):
            ref[a + LOW[level]:b + LOW[level]] = value
        return store

    def into_coarse(ref, level):
        def store(a, b, value):
            ref[a // 2 + LOW[level + 1]:b // 2 + LOW[level + 1]] = coarsen_field(value, 1 << level)
        return store

    def rows_of(ref, level):
        return lambda a, b: ref[a + LOW[level]:b + LOW[level]]

    def start(level, f_of, lo, hi):
        low = LOW[level]
        for a in range(lo, hi, 4):
            b = min(a + 4, hi)
            VA[level][a + low:b + low] = W[level][a + low:b + low] * f_of(a, b)

    def arr0(arr):
        return lambda a, b: e0[arr, a + 8:b + 8]

    coefficients(0, arr0(0), arr0(2), arr0(3), -6, 22)
    start(0, arr0(1), -6, 22)
    field(0, va0, into(vb0, 0), -5, 21, arr0(1), True)
    field(0, vb0, into_coarse(f1, 0), -4, 20, arr0(1), False)

    for comp, arr in enumerate((0, 2, 3)):
        lo, hi = (-4, 12) if arr == 0 else (-3, 11)
        m1[comp, lo + 4:hi + 4] = coarsen(e0[arr, 2 * lo + 8:2 * hi + 8], 1)

    def coarse1(comp):
        return lambda a, b: m1[comp, a + 4:b + 4]

    coefficients(1, coarse1(0), coarse1(1), coarse1(2), -3, 11)
    start(1, rows_of(f1, 1), -2, 10)
    field(1, va1, into(vb1, 1), -1, 9, rows_of(f1, 1), True)
    own2 = []

    def keep(a, b, value):
        own2.append(coarsen_field(value[:, 0], 2))

    field(1, vb1, keep, 0, 8, rows_of(f1, 1), False)
    part = lane & 3
    rf2[7] = jnp.where(part == 0, own2[0][0], jnp.where(part == 1, own2[0][1], jnp.where(part == 2, own2[1][0], own2[1][1])))
    for dx, dy in wide:
        send(rf2.at[7], rf2.at[7 - dx * 3 - dy], recv.at[2], beside(dx, dy), 12)

    pieces(tiles, 42, recv.at[0])
    quads = [(lane & ~3) + j for j in range(4)]

    def rows2(of, a, b):
        out = []
        for row in range(a, b):
            block = (row // 4 + 2) * 3
            main = of(block + 1)
            side = jnp.where(lane < 64, of(block + 2), of(block))
            out.append(jnp.stack([pick(main, quads[row % 4]), pick(side, quads[row % 4])]))
        return jnp.stack(out)

    def metric2(comp):
        def rows(a, b):
            got = rows2(lambda slot: rm2[slot, comp], a, b)
            return jnp.stack([jnp.stack([masked(got[n, p], 2, a + n, p) for p in range(2)]) for n in range(b - a)])
        return rows

    def metric3(comp):
        return lambda a, b: coarsen(metric2(comp)(2 * a, 2 * b), 4)

    coefficients(2, metric2(0), metric2(1), metric2(2), -7, 11)
    coefficients(3, metric3(0), metric3(1), metric3(2), -3, 5)

    pieces(tiles, 14, recv.at[2])
    pieces(lines, 45, recv.at[1])
    own4 = [jnp.where((lane & 8) == 0, ma[0, comp], ma[1, comp]) for comp in range(3)]
    for comp in range(3):
        mb[xc, yc, comp] = own4[comp]
    for target in plane:
        send(mb.at[xc, yc], mb.at[xc, yc], recv.at[3], target, 13)

    for a in range(-6, 10, 4):
        f2[a + 8:a + 12] = rows2(lambda slot: rf2[slot], a, a + 4)
    start(2, rows_of(f2, 2), -6, 10)
    field(2, va2, into(vb2, 2), -5, 9, rows_of(f2, 2), True)
    field(2, vb2, into_coarse(f3, 2), -4, 8, rows_of(f2, 2), False)
    start(3, rows_of(f3, 3), -2, 4)
    field(3, va3, into(vb3, 3), -1, 3, rows_of(f3, 3), True)
    own4f = []

    def keep4(a, b, value):
        own4f.append(coarsen_field(value[:, 0], 8))

    field(3, vb3, keep4, 0, 2, rows_of(f3, 3), False)
    fa[cc, pl.ds(zc, 1)] = spread_row(own4f[0][0])
    for target in column:
        mine = fa.at[cc, pl.ds(zc, 1)]
        send(mine, mine, recv.at[4], target, 14)

    rv3[7] = jnp.where(part == 0, vb3[4, 0], jnp.where(part == 1, vb3[5, 0], jnp.where(part == 2, f3[4, 0], f3[5, 0])))
    for dx, dy in wide:
        send(rv3.at[7], rv3.at[7 - dx * 3 - dy], recv.at[6], beside(dx, dy), 16)
    pieces(lines, 15, recv.at[4])
    fb[xc, yc] = jnp.where((lane & 8) == 0, fa[0], fa[1])
    for target in plane:
        send(fb.at[xc, yc], fb.at[xc, yc], recv.at[5], target, 15)

    for row in range(8):
        rv1[1, 4 + row] = jnp.where((lane & 1) == 0, vb1[4 + row, 0], f1[4 + row, 0])
    for dx in (-1, 0, 1):
        for dy in (-1, 0, 1):
            if (dx, dy) != (0, 0):
                a, b, c = ((4, 4, 12), (4, 8, 4), (8, 4, 0))[dx + 1]
                send(rv1.at[1, pl.ds(a, b)], rv1.at[1 - dy, pl.ds(c, b)], recv.at[7], beside(dx, dy), 17)

    pieces(tiles, 45, recv.at[3])
    four = 0.5 * 0.25**4
    column_y = lane & 63
    first_half = lane < 64
    whose = ((lane >> 4) - sub) & 7
    unturn = (lane + 16 * sub) & 127

    def whole(row_of):
        out = []
        for r in range(16):
            mixed = None
            for k in range(8):
                row = jnp.broadcast_to(row_of((r >> 3) + 2 * (k >> 2), k & 3, r & 7), (8, 128))
                mixed = row if k == 0 else jnp.where(whose == k, row, mixed)
            out.append(pick(mixed, unturn))
        return jnp.stack(out)

    def next_x(v):
        return jnp.concatenate([v[1:], jnp.where(first_half, pltpu.roll(v[0:1], 64, 2), 0.0)], axis=0)

    def last_x(v):
        return jnp.concatenate([jnp.where(first_half, 0.0, pltpu.roll(v[15:16], 64, 2)), v[:-1]], axis=0)

    def next_y(v):
        return pltpu.roll(v, 127, 2)

    def last_y(v):
        return pltpu.roll(v, 1, 2)

    mx, my, mz = [whole(lambda a, b, c, comp=comp: mb[a, b, comp, c:c + 1]) for comp in range(3)]
    ce, cw = four * (mx + next_x(mx)), four * (mx + last_x(mx))
    cn = four * (my + jnp.where(column_y == 63, 0.0, next_y(my)))
    cs = four * (my + jnp.where(column_y == 0, 0.0, last_y(my)))
    cu, cl = four * (mz + upper(mz)), four * (mz + lower(mz))
    c4[0] = ce
    c4[1] = cw
    c4[2] = jnp.where(column_y == 63, 0.0, cn)
    c4[3] = jnp.where(column_y == 0, 0.0, cs)
    c4[4] = cu
    c4[5] = cl
    c4[6] = ce + cw + cn + cs + cu + cl

    pieces(tiles, 14, recv.at[6])
    octs = [(lane & ~7) + j for j in range(4)]
    for d in range(-2, 3):
        block = (d + 2) * 3
        packed = (rv3[block + 1], jnp.where(first_half, rv3[block + 2], rv3[block]))
        inside = row_inside(3, 2 * d)
        for j in range(2):
            row = 2 * d + j
            for p_no in range(2):
                value = pick(packed[p_no], octs[j])
                if p_no == 1:
                    value = value * mask2
                va3[row + 4, p_no] = value if inside is None else value * inside
                if -3 <= row < 5:
                    f3[row + 4, p_no] = pick(packed[p_no], octs[2 + j])
    pieces(tiles, 15, recv.at[5])

    def total(x):
        tile = jnp.sum(x, axis=0)
        return jnp.sum(jnp.sum(tile, axis=0, keepdims=True), axis=1, keepdims=True)

    def image_of(p):
        out = c4[6] * p - c4[0] * next_x(p) - c4[1] * last_x(p)
        out = out - c4[2] * next_y(p) - c4[3] * last_y(p)
        return out - c4[4] * upper(p) - c4[5] * lower(p)

    r = whole(lambda a, b, c: fb[a, b, c:c + 1])
    p = q = v = rr = alpha = None
    for sweep in range(SWEEPS):
        image = image_of(r)
        new, power = total(r * r), total(r * image)
        if sweep == 0:
            p, q, alpha = r, image, new / power
            v = alpha * p
        else:
            beta = new / rr
            alpha = new / (power - beta * new / alpha)
            p = r + beta * p
            q = image + beta * q
            v = v + alpha * p
        rr = new
        if sweep + 1 < SWEEPS:
            r = r - alpha * q
    v4[...] = v

    for d in range(-2, 3):
        x = jnp.clip(gx + d, 0, NGX - 1)
        tile = v4[x & 15]
        half = (x >> 4) * 64
        main = pick(tile, half + gy * 8 + (lane >> 4))
        side = pick(tile, half + ((gy * 8 + jnp.where(first_half, 8, -8) + (lane >> 4)) & 63)) * mask2
        inside = row_inside(3, 2 * d)
        if inside is not None:
            main, side = main * inside, side * inside
        for row in (2 * d, 2 * d + 1):
            va3[row + 4, 0] = va3[row + 4, 0] + main
            va3[row + 4, 1] = va3[row + 4, 1] + side
    field(3, va3, into(vb3, 3), -3, 5, rows_of(f3, 3), True)
    field(3, vb3, into(va3, 3), -2, 4, rows_of(f3, 3), True)

    def refined(ref, level, a, b):
        x = ref[a + LOW[level]:b + LOW[level]]
        return jnp.stack([x, x], axis=1).reshape((2 * (b - a),) + x.shape[1:])

    def correct(level, a, b):
        low = LOW[level]
        for n in range(a, b, 4):
            m = min(n + 4, b)
            VA[level][n + low:m + low] = VB[level][n + low:m + low] + refined(VA[level + 1], level + 1, n // 2, m // 2)

    correct(2, -4, 8)
    field(2, va2, into(vb2, 2), -3, 7, rows_of(f2, 2), True)
    field(2, vb2, into(va2, 2), -2, 6, rows_of(f2, 2), True)

    pieces(tiles, 40, recv.at[7])
    evens, odds = lane & ~1, lane | 1
    for row in range(-4, 12):
        inside = row_inside(1, row)
        if inside is not None:
            value = pick(rv1[1, row + 4], evens)
            vb1[row + 4, 0] = value * inside
            f1[row + 4, 0] = pick(rv1[1, row + 4], odds)
        packed = jnp.where(lane < 64, rv1[2, row + 4], rv1[0, row + 4])
        value = pick(packed, evens) * mask0
        vb1[row + 4, 1] = value if inside is None else value * inside
        f1[row + 4, 1] = pick(packed, odds)
    correct(1, -4, 12)
    field(1, va1, into(vb1, 1), -3, 11, rows_of(f1, 1), True)
    field(1, vb1, into(va1, 1), -2, 10, rows_of(f1, 1), True)

    for a in range(-2, 9):
        lo = -3 if a == -2 else 2 * a
        hi = 2 * a + 2
        add = va1[a + 4]
        for row in range(lo, hi):
            va0[row + 8] = vb0[row + 8] + add
    va0[18 + 8] = vb0[18 + 8] + va1[9 + 4]
    field(0, va0, into(vb0, 0), -2, 18, arr0(1), True)

    def out_stream(a, b, value):
        va0[a + 8:b + 8] = value
        for row in range(max(a, 0), min(b, 16)):
            s_ref[pl.ds(row, 8, 16), :] = value[row - a, 0]

    def out_residual(a, b, value):
        for row in range(a, b):
            q_ref[pl.ds(row, 8, 16), :] = value[row - a, 0]

    field(0, vb0, out_stream, -1, 17, arr0(1), True)
    field(0, va0, out_residual, 0, 16, arr0(1), False)

    for copy in sends:
        copy.wait_send()
    for group, (kind, count) in enumerate(
            ((tiles, 42), (lines, 45), (tiles, 14), (tiles, 45), (lines, 15), (tiles, 15), (tiles, 14), (tiles, 40))):
        pieces(kind, count, ssem.at[10 + group])


def level_scratch():
    shapes = []
    for level in range(4):
        shapes.append(pltpu.VMEM((ROWS[level], 2, 8, 128), F32))
    return shapes


def on_device(vorticity, metric):
    depth, rows, columns = vorticity.shape
    tile = (8, 128)
    scratch = [
        pltpu.VMEM((4, 32, 2) + tile, F32), pltpu.VMEM((3, 16, 2) + tile, F32),
        pltpu.VMEM((4, 128, 128), jnp.bfloat16),
        pltpu.VMEM((depth * rows, columns), F32), pltpu.VMEM((3 * depth * rows, columns), F32),
        pltpu.SemaphoreType.DMA((2,)),
        pltpu.VMEM((4,) + tile, F32), pltpu.VMEM((4,) + tile, F32),
        pltpu.VMEM((8,) + tile, F32), pltpu.VMEM((8,) + tile, F32),
        pltpu.VMEM((15, 3) + tile, F32), pltpu.VMEM((15,) + tile, F32),
        pltpu.VMEM((2, 3) + tile, F32), pltpu.VMEM((4, 4, 3) + tile, F32),
        pltpu.VMEM((2,) + tile, F32), pltpu.VMEM((4, 4) + tile, F32),
        pltpu.VMEM((15,) + tile, F32), pltpu.VMEM((3, 16) + tile, F32),
        pltpu.VMEM((16,) + tile, F32), pltpu.VMEM((7, 16) + tile, F32),
    ]
    scratch += level_scratch()[1:]
    for _ in range(6):
        scratch += level_scratch()
    scratch += [pltpu.VMEM((45,) + tile, F32), pltpu.VMEM((45, 1, 128), F32)]
    scratch += [pltpu.SemaphoreType.DMA((18,)), pltpu.SemaphoreType.DMA((10,)), pltpu.SemaphoreType.DMA((8,))]
    flat = jax.ShapeDtypeStruct((depth * rows, columns), F32)
    vmem = pl.BlockSpec(memory_space=pltpu.VMEM)
    stream, residual = pl.pallas_call(
        kernel,
        out_shape=(flat, flat),
        in_specs=[pl.BlockSpec(memory_space=pl.ANY)] * 2,
        out_specs=(vmem, vmem),
        scratch_shapes=scratch,
        compiler_params=pltpu.CompilerParams(collective_id=0, has_side_effects=True, vmem_limit_bytes=48 * 1024 * 1024),
    )(vorticity.reshape(depth * rows, columns), metric.reshape(3 * depth * rows, columns))
    return stream.reshape(vorticity.shape), residual.reshape(vorticity.shape)


def solution(mesh):
    return jax.shard_map(
        on_device,
        mesh=mesh,
        in_specs=(P(None, "gx", "gy"), P(None, None, "gx", "gy")),
        out_specs=(P(None, "gx", "gy"), P(None, "gx", "gy")),
        check_vma=False,
    )
```

```python
import jax
import jax.numpy as jnp
from jax import lax
from jax.experimental import pallas as pl
from jax.experimental.pallas import tpu as pltpu
from jax.sharding import PartitionSpec as P

MESH = pl.DeviceIdType.MESH
NGX, NGY = 32, 8
OMEGA = 0.8
SPAN = 0.25**4
SWEEPS = 8
F32 = jnp.float32

LOW = (8, 4, 8, 4)
ROWS = (32, 16, 20, 10)


def lanes():
    return lax.broadcasted_iota(jnp.int32, (8, 128), 1)


def swap(x):
    return jnp.concatenate([x[:, 1:2], x[:, 0:1]], axis=1)


def north(x, step):
    turned = pltpu.roll(x, 128 - step, 3)
    return jnp.where(lanes() >= 128 - step, swap(turned), turned)


def south(x, step):
    turned = pltpu.roll(x, step, 3)
    return jnp.where(lanes() < step, swap(turned), turned)


def upper(x):
    return pltpu.roll(x, 7, x.ndim - 2)


def lower(x):
    return pltpu.roll(x, 1, x.ndim - 2)


def operate(v, cx, cy, cz, step):
    fx = cx * (v[:-1] - v[1:])
    mid = v[1:-1]
    fy = cy * (mid - north(mid, step))
    fz = cz * (mid - upper(mid))
    return (fx[1:] - fx[:-1]) + (fy - south(fy, step)) + (fz - lower(fz))


def coarsen_field(x, step):
    y = x.reshape((x.shape[0] // 2, 2) + x.shape[1:])
    both, axis = y[:, 0] + y[:, 1], x.ndim - 1
    other = jnp.where((lanes() & step) == 0, pltpu.roll(both, 128 - step, axis), pltpu.roll(both, step, axis))
    return 0.25 * (both + other)


def moved(x, matrix):
    first = x.astype(jnp.bfloat16)
    rest = x - first.astype(F32)
    second = rest.astype(jnp.bfloat16)
    third = (rest - second.astype(F32)).astype(jnp.bfloat16)
    terms = [jnp.dot(term, matrix, preferred_element_type=F32) for term in (first, second, third)]
    return terms[0] + (terms[1] + terms[2])


def pick(x, index):
    return jnp.take_along_axis(x, index, axis=1)


def kernel(f_ref, m_ref, s_ref, q_ref,
           e0, m1, pairs, f_in, m_in, in_sem, kr, kl, rkl, rkr, rm2, rf2, ma, mb, fa, fb, rv3, rv1, v4, c4,
           f1, f2, f3, w0, w1, w2, w3, cx0, cx1, cx2, cx3, cy0, cy1, cy2, cy3, cz0, cz1, cz2, cz3,
           va0, va1, va2, va3, vb0, vb1, vb2, vb3,
           tiles, lines, ssem, r1_sem, recv):
    gx, gy = lax.axis_index("gx"), lax.axis_index("gy")
    xc, zc = gx >> 3, gx & 7
    yc, cc = gy >> 1, gy & 1
    CX, CY, CZ, W = (cx0, cx1, cx2, cx3), (cy0, cy1, cy2, cy3), (cz0, cz1, cz2, cz3), (w0, w1, w2, w3)
    VA, VB = (va0, va1, va2, va3), (vb0, vb1, vb2, vb3)
    lane = lanes()
    sub = lax.broadcasted_iota(jnp.int32, (8, 128), 0)
    slot = lane >> 3

    def beside(dx, dy):
        return ((gx + dx + NGX) % NGX, (gy + dy + NGY) % NGY)

    wide = [(dx, dy) for dx in (-2, -1, 0, 1, 2) for dy in (-1, 0, 1) if (dx, dy) != (0, 0)]
    column = [(xc * 8 + (zc + dz) % 8, yc * 2 + (cc + dc) % 2) for dz in range(8) for dc in range(2) if (dz, dc) != (0, 0)]
    plane = [(((xc + dx) % 4) * 8 + zc, ((yc + dy) % 4) * 2 + cc) for dx in range(4) for dy in range(4) if (dx, dy) != (0, 0)]

    def pair_mean(total, step):
        return moved(total.reshape(-1, 128), pairs[step.bit_length() - 1]).reshape(total.shape)

    def coarsen(x, step):
        y = x.reshape((x.shape[0] // 2, 2) + x.shape[1:])
        return pair_mean(y[:, 0] + y[:, 1], step)

    barrier = pltpu.get_barrier_semaphore()
    everyone = [beside(dx, dy) for dx, dy in wide] + column + plane
    for target in everyone:
        pl.semaphore_signal(barrier, inc=1, device_id=target, device_id_type=MESH)

    def send(src, dst, sem, to, out):
        copy = pltpu.make_async_remote_copy(
            src_ref=src, dst_ref=dst, send_sem=ssem.at[out], recv_sem=sem, device_id=to, device_id_type=MESH)
        copy.start()
        return copy

    def pieces(kind, count, sem):
        ref = kind.at[pl.ds(0, count)]
        pltpu.make_async_copy(ref, ref, sem).wait()

    source = lax.broadcasted_iota(jnp.int32, (128, 128), 0)
    goal = lax.broadcasted_iota(jnp.int32, (128, 128), 1)

    def matrix_of(condition, value=1.0):
        return jnp.where(condition, value, 0.0).astype(jnp.bfloat16)

    loads = [pltpu.make_async_copy(m_ref, m_in, in_sem.at[0]), pltpu.make_async_copy(f_ref, f_in, in_sem.at[1])]
    for copy in loads:
        copy.start()
    for copy in loads:
        copy.wait()

    for row in range(16):
        for arr in range(4):
            if arr == 1:
                tile = f_in[pl.ds(row, 8, 16), :]
            else:
                tile = m_in[pl.ds((arr - 1 if arr else 0) * 128 + row, 8, 16), :]
            e0[arr, 8 + row, 0] = tile
    for k in range(4):
        right, left = jnp.zeros((8, 128), F32), jnp.zeros((8, 128), F32)
        for g in range(16):
            turned = pltpu.roll(e0[g % 4, 8 + 4 * k + g // 4, 0], (8 * g + 8) % 128, 1)
            right = jnp.where(slot == g, turned, right)
            left = jnp.where(slot == (g + 1) % 16, turned, left)
        kr[k] = right
        kl[k] = left

    turn = yc + 4 * (xc >> 1)

    def spread_row(tile):
        turned = pick(tile, 16 * (lane & 7))
        return jnp.sum(jnp.where(sub == (((lane >> 4) - turn) & 7), turned, 0.0), axis=0, keepdims=True)

    pl.semaphore_wait(barrier, len(everyone))

    sends = []
    east, west = beside(1, 0), beside(-1, 0)
    rest = pl.ds(1, 3)
    for side, (packed, into) in enumerate(((kr, rkl), (kl, rkr))):
        dy = 1 - 2 * side
        for n, (dx, a, b, c) in enumerate(((1, 2, 2, 0), (-1, 0, 2, 6), (0, 0, 4, 2))):
            at = 4 + 3 * side + n
            sends.append(send(packed.at[pl.ds(a, b)], into.at[pl.ds(c, b)], r1_sem.at[at], beside(dx, dy), at))
    sends.append(send(e0.at[0, pl.ds(16, 8), 0], e0.at[0, pl.ds(0, 8), 0], r1_sem.at[0], east, 0))
    sends.append(send(e0.at[0, pl.ds(8, 8), 0], e0.at[0, pl.ds(24, 8), 0], r1_sem.at[1], west, 1))
    sends.append(send(e0.at[rest, pl.ds(18, 6), 0], e0.at[rest, pl.ds(2, 6), 0], r1_sem.at[2], east, 2))
    sends.append(send(e0.at[rest, pl.ds(8, 6), 0], e0.at[rest, pl.ds(24, 6), 0], r1_sem.at[3], west, 3))
    for n in range(4):
        pairs[n] = matrix_of(jnp.logical_or(source == goal, source == (goal ^ (1 << n))), 0.25)
    for comp in range(3):
        arr = (0, 2, 3)[comp]
        m2 = coarsen(coarsen(e0[arr, 8:24, 0], 1), 2)
        m3 = coarsen(m2, 4)
        m4 = coarsen(m3, 8)
        part = lane & 3
        rm2[7, comp] = jnp.where(part == 0, m2[0], jnp.where(part == 1, m2[1], jnp.where(part == 2, m2[2], m2[3])))
        ma[cc, comp, pl.ds(zc, 1)] = spread_row(m4[0])

    for dx, dy in wide:
        send(rm2.at[7], rm2.at[7 - dx * 3 - dy], recv.at[0], beside(dx, dy), 10)
    for target in column:
        mine = ma.at[cc, pl.ds(0, 3), pl.ds(zc, 1)]
        send(mine, mine, recv.at[1], target, 11)
    for copy in sends:
        copy.wait_recv()

    even = (lane & 8) == 0
    for k in range(8):
        me = jnp.where(even, rkl[k], rkr[k])
        mo = jnp.where(even, rkr[k], rkl[k])
        for g in range(16):
            e0[g % 4, 4 * k + g // 4, 1] = pltpu.roll(me if g % 2 == 0 else mo, (120 - 8 * g) % 128, 1)

    has_left, has_right = gy > 0, gy < NGY - 1

    def side_mask(reach):
        inside = jnp.logical_or(jnp.logical_and(lane < reach, has_right), jnp.logical_and(lane >= 128 - reach, has_left))
        return inside.astype(F32)

    mask0, mask2 = side_mask(8), side_mask(64)

    def row_inside(level, row):
        own = 16 >> level
        if row < 0:
            need = -(row // own)
            return (gx >= need).astype(F32)
        if row >= own:
            return (gx + row // own <= NGX - 1).astype(F32)
        return None

    def masked(tile, level, row, part):
        side = mask0 if level < 2 else mask2
        scale = row_inside(level, row)
        if part == 1:
            tile = tile * side
        return tile if scale is None else tile * scale

    for arr in (0, 2, 3):
        for row in range(-8 if arr == 0 else -6, 24 if arr == 0 else 22):
            for part in range(2):
                if part == 1 or row < 0 or row >= 16:
                    e0[arr, row + 8, part] = masked(e0[arr, row + 8, part], 0, row, part)

    def coefficients(level, mx, my, mz, lo, hi):
        low, step = LOW[level], 1 << level
        half, spans = 0.5 * 0.25**level, 0.5 * SPAN
        for a in range(lo, hi, 4):
            b = min(a + 4, hi)
            x = mx(a - 1, b + 1)
            cx = half * (x[:-1] + x[1:])
            y = my(a, b)
            cy = half * (y + north(y, step))
            z = mz(a, b)
            cz = spans * (z + upper(z))
            CX[level][a - 1 + low:b + low] = cx
            CY[level][a + low:b + low] = cy
            CZ[level][a + low:b + low] = cz
            diag = cx[:-1] + cx[1:] + cy + south(cy, step) + cz + lower(cz)
            w = OMEGA / diag
            for row in range(a, b):
                for part in range(2):
                    tile = w[row - a, part]
                    side = mask0 if level < 2 else mask2
                    scale = row_inside(level, row)
                    if part == 1:
                        tile = jnp.where(side > 0, tile, 0.0)
                    if scale is not None:
                        tile = jnp.where(scale > 0, tile, 0.0)
                    W[level][row + low, part] = tile

    def field(level, source, target, lo, hi, f_of, relax, chunk=4):
        low, step = LOW[level], 1 << level
        for a in range(lo, hi, chunk):
            b = min(a + chunk, hi)
            v = source[a - 1 + low:b + 1 + low]
            left = f_of(a, b) - operate(
                v, CX[level][a - 1 + low:b + low], CY[level][a + low:b + low], CZ[level][a + low:b + low], step)
            target(a, b, v[1:-1] + W[level][a + low:b + low] * left if relax else left)

    def into(ref, level):
        def store(a, b, value):
            ref[a + LOW[level]:b + LOW[level]] = value
        return store

    def into_coarse(ref, level):
        def store(a, b, value):
            ref[a // 2 + LOW[level + 1]:b // 2 + LOW[level + 1]] = coarsen_field(value, 1 << level)
        return store

    def rows_of(ref, level):
        return lambda a, b: ref[a + LOW[level]:b + LOW[level]]

    def start(level, f_of, lo, hi):
        low = LOW[level]
        for a in range(lo, hi, 4):
            b = min(a + 4, hi)
            VA[level][a + low:b + low] = W[level][a + low:b + low] * f_of(a, b)

    def arr0(arr):
        return lambda a, b: e0[arr, a + 8:b + 8]

    coefficients(0, arr0(0), arr0(2), arr0(3), -6, 22)
    start(0, arr0(1), -6, 22)
    field(0, va0, into(vb0, 0), -5, 21, arr0(1), True)
    field(0, vb0, into_coarse(f1, 0), -4, 20, arr0(1), False)

    for comp, arr in enumerate((0, 2, 3)):
        lo, hi = (-4, 12) if arr == 0 else (-3, 11)
        m1[comp, lo + 4:hi + 4] = coarsen(e0[arr, 2 * lo + 8:2 * hi + 8], 1)

    def coarse1(comp):
        return lambda a, b: m1[comp, a + 4:b + 4]

    coefficients(1, coarse1(0), coarse1(1), coarse1(2), -3, 11)
    start(1, rows_of(f1, 1), -2, 10)
    field(1, va1, into(vb1, 1), -1, 9, rows_of(f1, 1), True)
    own2 = []

    def keep(a, b, value):
        own2.append(coarsen_field(value[:, 0], 2))

    field(1, vb1, keep, 0, 8, rows_of(f1, 1), False)
    part = lane & 3
    rf2[7] = jnp.where(part == 0, own2[0][0], jnp.where(part == 1, own2[0][1], jnp.where(part == 2, own2[1][0], own2[1][1])))
    for dx, dy in wide:
        send(rf2.at[7], rf2.at[7 - dx * 3 - dy], recv.at[2], beside(dx, dy), 12)

    pieces(tiles, 42, recv.at[0])
    quads = [(lane & ~3) + j for j in range(4)]

    def rows2(of, a, b):
        out = []
        for row in range(a, b):
            block = (row // 4 + 2) * 3
            main = of(block + 1)
            side = jnp.where(lane < 64, of(block + 2), of(block))
            out.append(jnp.stack([pick(main, quads[row % 4]), pick(side, quads[row % 4])]))
        return jnp.stack(out)

    def metric2(comp):
        def rows(a, b):
            got = rows2(lambda slot: rm2[slot, comp], a, b)
            return jnp.stack([jnp.stack([masked(got[n, p], 2, a + n, p) for p in range(2)]) for n in range(b - a)])
        return rows

    def metric3(comp):
        return lambda a, b: coarsen(metric2(comp)(2 * a, 2 * b), 4)

    coefficients(2, metric2(0), metric2(1), metric2(2), -7, 11)
    coefficients(3, metric3(0), metric3(1), metric3(2), -3, 5)

    pieces(tiles, 14, recv.at[2])
    pieces(lines, 45, recv.at[1])
    own4 = [jnp.where((lane & 8) == 0, ma[0, comp], ma[1, comp]) for comp in range(3)]
    for comp in range(3):
        mb[xc, yc, comp] = own4[comp]
    for target in plane:
        send(mb.at[xc, yc], mb.at[xc, yc], recv.at[3], target, 13)

    for a in range(-6, 10, 4):
        f2[a + 8:a + 12] = rows2(lambda slot: rf2[slot], a, a + 4)
    start(2, rows_of(f2, 2), -6, 10)
    field(2, va2, into(vb2, 2), -5, 9, rows_of(f2, 2), True)
    field(2, vb2, into_coarse(f3, 2), -4, 8, rows_of(f2, 2), False)
    start(3, rows_of(f3, 3), -2, 4)
    field(3, va3, into(vb3, 3), -1, 3, rows_of(f3, 3), True)
    own4f = []

    def keep4(a, b, value):
        own4f.append(coarsen_field(value[:, 0], 8))

    field(3, vb3, keep4, 0, 2, rows_of(f3, 3), False)
    fa[cc, pl.ds(zc, 1)] = spread_row(own4f[0][0])
    for target in column:
        mine = fa.at[cc, pl.ds(zc, 1)]
        send(mine, mine, recv.at[4], target, 14)

    rv3[7] = jnp.where(part == 0, vb3[4, 0], jnp.where(part == 1, vb3[5, 0], jnp.where(part == 2, f3[4, 0], f3[5, 0])))
    for dx, dy in wide:
        send(rv3.at[7], rv3.at[7 - dx * 3 - dy], recv.at[6], beside(dx, dy), 16)
    pieces(lines, 15, recv.at[4])
    fb[xc, yc] = jnp.where((lane & 8) == 0, fa[0], fa[1])
    for target in plane:
        send(fb.at[xc, yc], fb.at[xc, yc], recv.at[5], target, 15)

    for row in range(8):
        rv1[1, 4 + row] = jnp.where((lane & 1) == 0, vb1[4 + row, 0], f1[4 + row, 0])
    for dx in (-1, 0, 1):
        for dy in (-1, 0, 1):
            if (dx, dy) != (0, 0):
                a, b, c = ((4, 4, 12), (4, 8, 4), (8, 4, 0))[dx + 1]
                send(rv1.at[1, pl.ds(a, b)], rv1.at[1 - dy, pl.ds(c, b)], recv.at[7], beside(dx, dy), 17)

    pieces(tiles, 45, recv.at[3])
    four = 0.5 * 0.25**4
    column_y = lane & 63
    first_half = lane < 64
    whose = ((lane >> 4) - sub) & 7
    unturn = (lane + 16 * sub) & 127

    def whole(row_of):
        out = []
        for r in range(16):
            mixed = None
            for k in range(8):
                row = jnp.broadcast_to(row_of((r >> 3) + 2 * (k >> 2), k & 3, r & 7), (8, 128))
                mixed = row if k == 0 else jnp.where(whose == k, row, mixed)
            out.append(pick(mixed, unturn))
        return jnp.stack(out)

    def next_x(v):
        return jnp.concatenate([v[1:], jnp.where(first_half, pltpu.roll(v[0:1], 64, 2), 0.0)], axis=0)

    def last_x(v):
        return jnp.concatenate([jnp.where(first_half, 0.0, pltpu.roll(v[15:16], 64, 2)), v[:-1]], axis=0)

    def next_y(v):
        return pltpu.roll(v, 127, 2)

    def last_y(v):
        return pltpu.roll(v, 1, 2)

    mx, my, mz = [whole(lambda a, b, c, comp=comp: mb[a, b, comp, c:c + 1]) for comp in range(3)]
    ce, cw = four * (mx + next_x(mx)), four * (mx + last_x(mx))
    cn = four * (my + jnp.where(column_y == 63, 0.0, next_y(my)))
    cs = four * (my + jnp.where(column_y == 0, 0.0, last_y(my)))
    cu, cl = four * (mz + upper(mz)), four * (mz + lower(mz))
    c4[0] = ce
    c4[1] = cw
    c4[2] = jnp.where(column_y == 63, 0.0, cn)
    c4[3] = jnp.where(column_y == 0, 0.0, cs)
    c4[4] = cu
    c4[5] = cl
    c4[6] = ce + cw + cn + cs + cu + cl

    pieces(tiles, 14, recv.at[6])
    octs = [(lane & ~7) + j for j in range(4)]
    for d in range(-2, 3):
        block = (d + 2) * 3
        packed = (rv3[block + 1], jnp.where(first_half, rv3[block + 2], rv3[block]))
        inside = row_inside(3, 2 * d)
        for j in range(2):
            row = 2 * d + j
            for p_no in range(2):
                value = pick(packed[p_no], octs[j])
                if p_no == 1:
                    value = value * mask2
                va3[row + 4, p_no] = value if inside is None else value * inside
                if -3 <= row < 5:
                    f3[row + 4, p_no] = pick(packed[p_no], octs[2 + j])
    pieces(tiles, 15, recv.at[5])

    def total(x):
        tile = jnp.sum(x, axis=0)
        return jnp.sum(jnp.sum(tile, axis=0, keepdims=True), axis=1, keepdims=True)

    def image_of(p):
        out = c4[6] * p - c4[0] * next_x(p) - c4[1] * last_x(p)
        out = out - c4[2] * next_y(p) - c4[3] * last_y(p)
        return out - c4[4] * upper(p) - c4[5] * lower(p)

    r = whole(lambda a, b, c: fb[a, b, c:c + 1])
    p = q = v = rr = alpha = None
    for sweep in range(SWEEPS):
        image = image_of(r)
        new, power = total(r * r), total(r * image)
        if sweep == 0:
            p, q, alpha = r, image, new / power
            v = alpha * p
        else:
            beta = new / rr
            alpha = new / (power - beta * new / alpha)
            p = r + beta * p
            q = image + beta * q
            v = v + alpha * p
        rr = new
        if sweep + 1 < SWEEPS:
            r = r - alpha * q
    v4[...] = v

    for d in range(-2, 3):
        x = jnp.clip(gx + d, 0, NGX - 1)
        tile = v4[x & 15]
        half = (x >> 4) * 64
        main = pick(tile, half + gy * 8 + (lane >> 4))
        side = pick(tile, half + ((gy * 8 + jnp.where(first_half, 8, -8) + (lane >> 4)) & 63)) * mask2
        inside = row_inside(3, 2 * d)
        if inside is not None:
            main, side = main * inside, side * inside
        for row in (2 * d, 2 * d + 1):
            va3[row + 4, 0] = va3[row + 4, 0] + main
            va3[row + 4, 1] = va3[row + 4, 1] + side
    field(3, va3, into(vb3, 3), -3, 5, rows_of(f3, 3), True)
    field(3, vb3, into(va3, 3), -2, 4, rows_of(f3, 3), True)

    def refined(ref, level, a, b):
        x = ref[a + LOW[level]:b + LOW[level]]
        return jnp.stack([x, x], axis=1).reshape((2 * (b - a),) + x.shape[1:])

    def correct(level, a, b):
        low = LOW[level]
        for n in range(a, b, 4):
            m = min(n + 4, b)
            VA[level][n + low:m + low] = VB[level][n + low:m + low] + refined(VA[level + 1], level + 1, n // 2, m // 2)

    correct(2, -4, 8)
    field(2, va2, into(vb2, 2), -3, 7, rows_of(f2, 2), True)
    field(2, vb2, into(va2, 2), -2, 6, rows_of(f2, 2), True)

    pieces(tiles, 40, recv.at[7])
    evens, odds = lane & ~1, lane | 1
    for row in range(-4, 12):
        inside = row_inside(1, row)
        if inside is not None:
            value = pick(rv1[1, row + 4], evens)
            vb1[row + 4, 0] = value * inside
            f1[row + 4, 0] = pick(rv1[1, row + 4], odds)
        packed = jnp.where(lane < 64, rv1[2, row + 4], rv1[0, row + 4])
        value = pick(packed, evens) * mask0
        vb1[row + 4, 1] = value if inside is None else value * inside
        f1[row + 4, 1] = pick(packed, odds)
    correct(1, -4, 12)
    field(1, va1, into(vb1, 1), -3, 11, rows_of(f1, 1), True)
    field(1, vb1, into(va1, 1), -2, 10, rows_of(f1, 1), True)

    for a in range(-2, 9):
        lo = -3 if a == -2 else 2 * a
        hi = 2 * a + 2
        add = va1[a + 4]
        for row in range(lo, hi):
            va0[row + 8] = vb0[row + 8] + add
    va0[18 + 8] = vb0[18 + 8] + va1[9 + 4]
    field(0, va0, into(vb0, 0), -2, 18, arr0(1), True)

    def out_stream(a, b, value):
        va0[a + 8:b + 8] = value
        for row in range(max(a, 0), min(b, 16)):
            s_ref[pl.ds(row, 8, 16), :] = value[row - a, 0]

    def out_residual(a, b, value):
        for row in range(a, b):
            q_ref[pl.ds(row, 8, 16), :] = value[row - a, 0]

    field(0, vb0, out_stream, -1, 17, arr0(1), True)
    field(0, va0, out_residual, 0, 16, arr0(1), False)

    for copy in sends:
        copy.wait_send()
    for group, (kind, count) in enumerate(
            ((tiles, 42), (lines, 45), (tiles, 14), (tiles, 45), (lines, 15), (tiles, 15), (tiles, 14), (tiles, 40))):
        pieces(kind, count, ssem.at[10 + group])


def level_scratch():
    shapes = []
    for level in range(4):
        shapes.append(pltpu.VMEM((ROWS[level], 2, 8, 128), F32))
    return shapes


def on_device(vorticity, metric):
    depth, rows, columns = vorticity.shape
    tile = (8, 128)
    scratch = [
        pltpu.VMEM((4, 32, 2) + tile, F32), pltpu.VMEM((3, 16, 2) + tile, F32),
        pltpu.VMEM((4, 128, 128), jnp.bfloat16),
        pltpu.VMEM((depth * rows, columns), F32), pltpu.VMEM((3 * depth * rows, columns), F32),
        pltpu.SemaphoreType.DMA((2,)),
        pltpu.VMEM((4,) + tile, F32), pltpu.VMEM((4,) + tile, F32),
        pltpu.VMEM((8,) + tile, F32), pltpu.VMEM((8,) + tile, F32),
        pltpu.VMEM((15, 3) + tile, F32), pltpu.VMEM((15,) + tile, F32),
        pltpu.VMEM((2, 3) + tile, F32), pltpu.VMEM((4, 4, 3) + tile, F32),
        pltpu.VMEM((2,) + tile, F32), pltpu.VMEM((4, 4) + tile, F32),
        pltpu.VMEM((15,) + tile, F32), pltpu.VMEM((3, 16) + tile, F32),
        pltpu.VMEM((16,) + tile, F32), pltpu.VMEM((7, 16) + tile, F32),
    ]
    scratch += level_scratch()[1:]
    for _ in range(6):
        scratch += level_scratch()
    scratch += [pltpu.VMEM((45,) + tile, F32), pltpu.VMEM((45, 1, 128), F32)]
    scratch += [pltpu.SemaphoreType.DMA((18,)), pltpu.SemaphoreType.DMA((10,)), pltpu.SemaphoreType.DMA((8,))]
    flat = jax.ShapeDtypeStruct((depth * rows, columns), F32)
    vmem = pl.BlockSpec(memory_space=pltpu.VMEM)
    stream, residual = pl.pallas_call(
        kernel,
        out_shape=(flat, flat),
        in_specs=[pl.BlockSpec(memory_space=pl.ANY)] * 2,
        out_specs=(vmem, vmem),
        scratch_shapes=scratch,
        compiler_params=pltpu.CompilerParams(collective_id=0, has_side_effects=True, vmem_limit_bytes=48 * 1024 * 1024),
    )(vorticity.reshape(depth * rows, columns), metric.reshape(3 * depth * rows, columns))
    return stream.reshape(vorticity.shape), residual.reshape(vorticity.shape)


def solution(mesh):
    return jax.shard_map(
        on_device,
        mesh=mesh,
        in_specs=(P(None, "gx", "gy"), P(None, None, "gx", "gy")),
        out_specs=(P(None, "gx", "gy"), P(None, "gx", "gy")),
        check_vma=False,
    )
```
